512 devices in a mesh: dp: 32 (over y, z_lo, core), shard: 16 (over z_hi, x).
Axes of the slice: x: 4, y: 4, z: 16 (z_hi: 4, z_lo: 4; z = z_hi * 4 + z_lo), core: 2. Of those that a mesh axis runs over, the one named last changes fastest.
Arguments:
- layer_input: bfloat16 [16384, 8192], P('dp', 'shard'), may hold values from -6 to 6
- out_grad: bfloat16 [16384, 14336], P('dp', 'shard'), may hold values from -48 to 48
- projector: bfloat16 [8192, 1024], P(('dp', 'shard')), may hold values from -0.0625 to 0.0625
- first_moment: float32 [1024, 14336], P('dp', 'shard'), may hold values from -1.75 to 1.75
- second_moment: float32 [1024, 14336], P('dp', 'shard'), may hold values from 0.05 to 0.5
- doc_ids: int32 [16384], P('dp'), may hold values from 0 to 31, as said below
Outputs:
- new_first: float32 [1024, 14336], P('dp', 'shard')
- new_second: float32 [1024, 14336], P('dp', 'shard')
- update: bfloat16 [8192, 14336], P('dp', 'shard')
The draws below stay inside these ranges and needn't reach their ends.
Inputs may be any that keep to these rules, and one draw needn't show every extreme that they name: `doc_ids`: numbers never fall along the tokens; every number from 0 to 31 occurs, each on 256 tokens or more.
All inputs are finite; a program needn't handle non-finite values.
Results may differ from the reference program's by a relative error of at most 0.0055.
Values may be sent and summed in bfloat16 or wider, within the bound.
A program may use at most 64 MiB of HBM per device.

```python
import math
import jax
import jax.numpy as jnp
from jax import lax

D = 8192
FF = 14336
R = 1024
TOK_DP = 512
TOKENS = 16384
DOCS = 32


def draw_doc_ids(key, part):
    key = jax.random.fold_in(key, 7)
    shortest = TOK_DP // 2
    leftover = TOKENS - DOCS * shortest
    cut_points = jnp.sort(jax.random.randint(key, (DOCS - 1,), 0, leftover + 1))
    cut_points = cut_points.at[0].set(0)
    doc_starts = (jnp.arange(1, DOCS, dtype=jnp.int32) * shortest + cut_points).astype(jnp.int32)
    positions = jnp.arange(TOKENS, dtype=jnp.int32)
    return jnp.sum((positions[:, None] >= doc_starts[None, :]).astype(jnp.int32), axis=1).astype(jnp.int32)


def steps_of(stream_key, shape, cuts, low, largest):
    def one(axis_at, shards_of):
        draws = jax.random.uniform(jax.random.fold_in(jax.random.fold_in(stream_key, 6), axis_at), (shards_of,), jnp.float32, low / len(cuts), largest / len(cuts))
        return jnp.repeat(jnp.exp(draws), shape[axis_at] // shards_of).reshape((-1,) + (1,) * (len(shape) - axis_at - 1))

    level = one(*cuts[0])
    for cut in cuts[1:]:
        level = level * one(*cut)
    return level


def centred(stream_key, dims, deviation, reach, split=(), kind=jnp.bfloat16):
    loudness = steps_of(stream_key, dims, split, -0.22, 0.18) if split else 1.0
    drawn = jax.random.normal(stream_key, dims, jnp.float32) * deviation * loudness
    return jnp.minimum(jnp.maximum(drawn, -reach), reach).astype(kind)


def setup_inputs(seed: int = 0) -> dict:
    arg_keys = jax.random.split(jax.random.key(seed), 7)
    return {
        "layer_input": centred(arg_keys[0], (TOKENS, D), 1.0, 6.0, ((0, 32), (1, 16))),
        "out_grad": centred(arg_keys[1], (TOKENS, FF), 8.0, 48.0, ((0, 32), (1, 16))),
        "projector": centred(arg_keys[2], (D, R), D ** -0.5, 0.0625, ((0, 512),)),
        "first_moment": centred(arg_keys[3], (R, FF), 0.3, 1.75, ((0, 32), (1, 16)), jnp.float32),
        "second_moment": jnp.clip(jnp.exp(math.log(0.5) - 2.3025851 * jax.random.uniform(arg_keys[4], (R, FF), jnp.float32) ** steps_of(arg_keys[4], (R, FF), ((0, 32), (1, 16)), -0.2, 0.2)), 0.05, 0.5),
        "doc_ids": draw_doc_ids(jax.random.fold_in(arg_keys[6], 71), 0),
    }


beta_first = 0.9
beta_second = 0.95
bias_first = 1.0 - beta_first ** 2
bias_second = 1.0 - beta_second ** 2
epsilon = 1e-08

def adam_step(first_moment, second_moment, gradient):
    new_first = beta_first * first_moment + (1.0 - beta_first) * gradient
    new_second = beta_second * second_moment + (1.0 - beta_second) * (gradient * gradient)
    direction = (new_first / bias_first / (jnp.sqrt(new_second / bias_second) + epsilon)).astype(jnp.bfloat16)
    return (new_first, new_second, direction)

def reference(layer_input, out_grad, projector, first_moment, second_moment, doc_ids):
    doc_match = (doc_ids[:, None] == jnp.arange(DOCS, dtype=jnp.int32)[None, :]).astype(jnp.float32)
    lengths = lax.optimization_barrier(jnp.sum(doc_match, axis=0))
    token_weight = lax.optimization_barrier(jnp.sum(doc_match * (1.0 / lengths)[None, :], axis=1))
    projected = jnp.dot(layer_input, projector, preferred_element_type=jnp.float32)
    weighted = (projected * token_weight[:, None]).astype(jnp.bfloat16)
    gradient = jnp.dot(weighted.T, out_grad, preferred_element_type=jnp.float32)
    new_first, new_second, direction = adam_step(first_moment, second_moment, gradient)
    update = jnp.dot(projector, direction, preferred_element_type=jnp.float32).astype(jnp.bfloat16)
    return (new_first, new_second, update)
```

```python
import jax
import jax.numpy as jnp
from jax import lax
from jax.experimental import pallas as pl
from jax.experimental.pallas import tpu as pltpu
from jax.sharding import PartitionSpec as P

MESH = pl.DeviceIdType.MESH
BF = jnp.bfloat16
F32 = jnp.float32

beta_first = 0.9
beta_second = 0.95
bias_first = 1.0 - beta_first**2
bias_second = 1.0 - beta_second**2
epsilon = 1e-08

TOK, FEAT, RANK, FF, ROWS = 512, 512, 1024, 896, 16
T = 4
CHUNK = TOK // T
SUB = CHUNK // 4
QUARTER = RANK // 4
MOM = 32
WIDTHS = (384, 512)
STARTS = tuple(sum(WIDTHS[:j]) for j in range(len(WIDTHS)))
N_SEM = 160


def kernel(x_hbm, g_hbm, p_hbm, m_hbm, v_hbm, ids_ref, m_out, v_out, u_out, *scratch):
    (
        x_in, g_in, m_in, v_in, rows_in, rows_up,
        part32, part, x_got, xsum32, xsum, z_got, wide, wide_t,
        count, count_got,
        loc_sem, out_sem, send_sem, recv_sem,
    ) = scratch[:20]
    per_chunk = [scratch[20 + 11 * j : 20 + 11 * (j + 1)] for j in range(len(WIDTHS))]

    d, s = lax.axis_index("dp"), lax.axis_index("shard")
    core = lax.rem(d, 2)
    zl = lax.rem(lax.div(d, 2), 4)
    y = lax.div(d, 8)
    x = lax.rem(s, 4)
    zh = lax.div(s, 4)

    def device(y=y, zl=zl, core=core, zh=zh, x=x):
        return ((y * 4 + zl) * 2 + core, zh * 4 + x)

    def up(value, k):
        return lax.rem(value + k, 4)

    other = 1 - core
    x_peers = [up(x, k) for k in (1, 3, 2)]
    y_peers = [up(y, k) for k in (1, 3, 2)]
    zl_peers = [up(zl, k) for k in (1, 3, 2)]
    zh_peers = [up(zh, k) for k in (1, 3, 2)]

    used = [0]
    sent = []

    def send(src, dst, to):
        i = used[0]
        used[0] += 1
        cp = pltpu.make_async_remote_copy(
            src_ref=src, dst_ref=dst, send_sem=send_sem.at[i], recv_sem=recv_sem.at[i],
            device_id=to, device_id_type=MESH,
        )
        cp.start()
        sent.append(cp)
        return cp

    def arrive(cps):
        for cp in cps:
            cp.wait_recv()

    own_rows = pltpu.make_async_copy(p_hbm, rows_up.at[zh, x], loc_sem.at[0])
    loads = [
        pltpu.make_async_copy(x_hbm, x_in, loc_sem.at[1]),
        pltpu.make_async_copy(g_hbm, g_in, loc_sem.at[2]),
        pltpu.make_async_copy(m_hbm, m_in, loc_sem.at[3]),
        pltpu.make_async_copy(v_hbm, v_in, loc_sem.at[4]),
    ]
    own_rows.start()
    for cp in loads:
        cp.start()

    partner = device(y=zh, zl=x, zh=y, x=zl)
    moves = jnp.logical_or(x != zl, y != zh)
    barrier = pltpu.get_barrier_semaphore()
    greet = [device(core=other)]
    greet += [device(x=p) for p in x_peers] + [device(y=p) for p in y_peers]
    greet += [device(zl=p) for p in zl_peers] + [device(zh=p) for p in zh_peers]
    for to in greet:
        pl.semaphore_signal(barrier, inc=1, device_id=to, device_id_type=MESH)

    @pl.when(moves)
    def _():
        pl.semaphore_signal(barrier, inc=1, device_id=partner, device_id_type=MESH)

    ids = jnp.transpose(jnp.broadcast_to(ids_ref[...], (128, TOK)))
    match = ids == lax.broadcasted_iota(jnp.int32, (TOK, 128), 1)
    counted = jnp.sum(match.astype(F32), axis=0, keepdims=True)
    count[0] = jnp.broadcast_to(counted, (8, 128))

    own_rows.wait()
    pl.semaphore_wait(barrier, len(greet) + moves.astype(jnp.int32))

    hop = used[0]
    used[0] += 1

    def hop_copy():
        return pltpu.make_async_remote_copy(
            src_ref=rows_up.at[zh, x], dst_ref=rows_in.at[core, zh, x],
            send_sem=send_sem.at[hop], recv_sem=recv_sem.at[hop],
            device_id=partner, device_id_type=MESH,
        )

    @pl.when(moves)
    def _():
        hop_copy().start()

    cp_c = [send(count.at[0], count_got.at[0], device(core=other))]

    @pl.when(jnp.logical_not(moves))
    def _():
        rows_in[core, zh, x] = rows_up[zh, x]

    @pl.when(moves)
    def _():
        hop_copy().wait_recv()

    cps = [send(rows_in.at[core, y, zl], rows_in.at[core, y, zl], device(zl=p)) for p in zl_peers]
    arrive(cp_c)
    count[1] = count[0] + count_got[0]
    cp_c = [send(count.at[1], count_got.at[1 + k], device(zl=p)) for k, p in enumerate(zl_peers)]
    arrive(cps)
    cps = [send(rows_in.at[core, y], rows_in.at[core, y], device(y=p)) for p in y_peers]
    arrive(cp_c)
    count[2] = count[1] + count_got[1] + count_got[2] + count_got[3]
    cp_c = [send(count.at[2], count_got.at[4 + k], device(y=p)) for k, p in enumerate(y_peers)]
    arrive(cps)
    cps = [send(rows_in.at[core], rows_in.at[core], device(core=other))]
    arrive(cp_c)
    lengths = count[2] + count_got[4] + count_got[5] + count_got[6]
    inverse = 1.0 / lengths[0:1]
    for cp in loads:
        cp.wait()
    arrive(cps)

    rhs = rows_in[...].reshape(FEAT, RANK)
    got_x, got_z, all_z, all_x = {}, {}, {}, {}

    def project(t):
        value = jnp.dot(x_in[pl.ds(t * CHUNK, CHUNK)], rhs, preferred_element_type=F32)
        for q in range(4):
            block = value[:, q * QUARTER : (q + 1) * QUARTER].reshape(4, SUB, QUARTER)
            part32[t, :, q] = block
            part[t, :, q] = block.astype(BF)
        got_x[t] = [
            send(part.at[t, p], x_got.at[t, k], device(x=p)) for k, p in enumerate(x_peers)
        ]

    def sum_x(t):
        arrive(got_x[t])
        total = part32[t, x]
        for k in range(3):
            total = total + x_got[t, k].astype(F32)
        xsum32[t] = total
        xsum[t] = total.astype(BF)
        got_z[t] = [
            send(xsum.at[t, p], z_got.at[t, k], device(zh=p)) for k, p in enumerate(zh_peers)
        ]

    def sum_z(t):
        arrive(got_z[t])
        total = xsum32[t, zh]
        for k in range(3):
            total = total + z_got[t, k].astype(F32)
        here = ids_of(t) == lax.broadcasted_iota(jnp.int32, (SUB, 128), 1)
        weight = jnp.sum(jnp.where(here, inverse, 0.0), axis=1, keepdims=True)
        wide[t, x, zh] = (total * weight).astype(BF)
        all_z[t] = [
            send(wide.at[t, x, zh], wide.at[t, x, zh], device(zh=p)) for p in zh_peers
        ]

    def ids_of(t):
        return part_ids[t, x]

    def gather_x(t):
        arrive(all_z[t])
        all_x[t] = [send(wide.at[t, x], wide.at[t, x], device(x=p)) for p in x_peers]

    def turn(t):
        arrive(all_x[t])
        for q in range(4):
            block = wide[t, :, q].reshape(CHUNK, QUARTER)
            block = jnp.transpose(block)
            for b in range(8):
                wide_t[b % 2, q * 4 + b // 2, :, t * CHUNK : (t + 1) * CHUNK] = block[
                    b * MOM : (b + 1) * MOM
                ]

    part_ids = scratch[-1]
    part_ids[...] = ids.reshape(T, 4, SUB, 128)
    stages = (project, sum_x, sum_z, gather_x, turn)
    for t in range(T):
        project(t)
    for step in range(T + 3):
        for stage in (1, 2, 3, 4):
            t = step - (stage - 1)
            if 0 <= t < T:
                stages[stage](t)

    up_z = [send(rows_up.at[zh, x], rows_up.at[zh, x], device(zh=p)) for p in zh_peers]
    up_x = []
    outs = []
    got = {}

    def gradient(j):
        g_own, g_peer, c_got = per_chunk[j][0:3]
        cols = pl.ds(STARTS[j], WIDTHS[j])
        lhs = wide_t[other].reshape(RANK // 2, TOK)
        value = jnp.dot(lhs, g_in[:, cols], preferred_element_type=F32)
        g_peer[...] = value.astype(BF).reshape(4, 4, MOM, WIDTHS[j])
        got["c", j] = [send(g_peer, c_got, device(core=other))]
        lhs = wide_t[core].reshape(RANK // 2, TOK)
        value = jnp.dot(lhs, g_in[:, cols], preferred_element_type=F32)
        g_own[...] = value.reshape(4, 4, MOM, WIDTHS[j])

    def sum_core(j):
        g_own, _, c_got, ysum, y_got = per_chunk[j][0:5]
        arrive(got["c", j])
        for k, p in enumerate(y_peers):
            ysum[k] = (g_own[p] + c_got[p].astype(F32)).astype(BF)
            got["y", j, k] = [send(ysum.at[k], y_got.at[k], device(y=p))]

    def sum_y(j):
        g_own, _, c_got, ysum, y_got, zsum32, zsum, l_got = per_chunk[j][0:8]
        total = g_own[y] + c_got[y].astype(F32)
        for k in range(3):
            arrive(got["y", j, k])
            total = total + y_got[k].astype(F32)
        zsum32[...] = total
        zsum[...] = total.astype(BF)
        got["l", j] = [
            send(zsum.at[p], l_got.at[k], device(zl=p)) for k, p in enumerate(zl_peers)
        ]

    def adam(j):
        zsum32, _, l_got, full, m_new, v_new = per_chunk[j][5:11]
        cols = pl.ds(STARTS[j], WIDTHS[j])
        arrive(got["l", j])
        grad = zsum32[zl]
        for k in range(3):
            grad = grad + l_got[k].astype(F32)
        first = beta_first * m_in[:, cols] + (1.0 - beta_first) * grad
        second = beta_second * v_in[:, cols] + (1.0 - beta_second) * (grad * grad)
        way = first / bias_first / (jnp.sqrt(second / bias_second) + epsilon)
        full[y, zl, core] = way.astype(BF)
        got["dl", j] = [
            send(full.at[y, zl, core], full.at[y, zl, core], device(zl=p)) for p in zl_peers
        ]
        m_new[...] = first
        v_new[...] = second
        for value, out in ((m_new, m_out), (v_new, v_out)):
            cp = pltpu.make_async_copy(value, out.at[:, cols], out_sem.at[len(outs)])
            cp.start()
            outs.append(cp)

    def gather_y(j):
        full = per_chunk[j][8]
        arrive(got["dl", j])
        got["dy", j] = [
            send(full.at[y, :, core], full.at[y, :, core], device(y=p)) for p in y_peers
        ]

    def gather_core(j):
        full = per_chunk[j][8]
        arrive(got["dy", j])
        got["dc", j] = [send(full.at[:, :, core], full.at[:, :, core], device(core=other))]

    def update(j):
        full, u_new = per_chunk[j][8], u_parts[j]
        cols = pl.ds(STARTS[j], WIDTHS[j])
        arrive(got["dc", j])
        lhs = rows_up[...].reshape(256, RANK)
        value = jnp.dot(lhs, full[...].reshape(RANK, WIDTHS[j]), preferred_element_type=F32)
        u_new[...] = value.astype(BF)
        cp = pltpu.make_async_copy(u_new, u_out.at[:, cols], out_sem.at[len(outs)])
        cp.start()
        outs.append(cp)

    u_parts = scratch[20 + 11 * len(WIDTHS) : 20 + 12 * len(WIDTHS)]
    stages = (gradient, sum_core, sum_y, adam, gather_y, gather_core, update)
    n = len(WIDTHS)
    for step in range(n + len(stages) - 1):
        for stage in range(len(stages)):
            j = step - stage
            if 0 <= j < n:
                if stage == 3 and j == 0:
                    arrive(up_z)
                    up_x += [
                        send(rows_up.at[:, x], rows_up.at[:, x], device(x=p)) for p in x_peers
                    ]
                if stage == 6 and j == 0:
                    arrive(up_x)
                stages[stage](j)

    @pl.when(moves)
    def _():
        hop_copy().wait_send()

    for cp in sent:
        cp.wait_send()
    for cp in outs:
        cp.wait()


def local(layer_input, out_grad, projector, first_moment, second_moment, doc_ids):
    scratch = [
        pltpu.VMEM((TOK, FEAT), BF),
        pltpu.VMEM((TOK, FF), BF),
        pltpu.VMEM((MOM, FF), F32),
        pltpu.VMEM((MOM, FF), F32),
        pltpu.VMEM((2, 4, 4, ROWS, RANK), BF),
        pltpu.VMEM((4, 4, ROWS, RANK), BF),
        pltpu.VMEM((T, 4, 4, SUB, QUARTER), F32),
        pltpu.VMEM((T, 4, 4, SUB, QUARTER), BF),
        pltpu.VMEM((T, 3, 4, SUB, QUARTER), BF),
        pltpu.VMEM((T, 4, SUB, QUARTER), F32),
        pltpu.VMEM((T, 4, SUB, QUARTER), BF),
        pltpu.VMEM((T, 3, SUB, QUARTER), BF),
        pltpu.VMEM((T, 4, 4, SUB, QUARTER), BF),
        pltpu.VMEM((2, 16, MOM, TOK), BF),
        pltpu.VMEM((3, 8, 128), F32),
        pltpu.VMEM((7, 8, 128), F32),
        pltpu.SemaphoreType.DMA((5,)),
        pltpu.SemaphoreType.DMA((3 * len(WIDTHS),)),
        pltpu.SemaphoreType.DMA((N_SEM,)),
        pltpu.SemaphoreType.DMA((N_SEM,)),
    ]
    for w in WIDTHS:
        scratch += [
            pltpu.VMEM((4, 4, MOM, w), F32),
            pltpu.VMEM((4, 4, MOM, w), BF),
            pltpu.VMEM((4, 4, MOM, w), BF),
            pltpu.VMEM((3, 4, MOM, w), BF),
            pltpu.VMEM((3, 4, MOM, w), BF),
            pltpu.VMEM((4, MOM, w), F32),
            pltpu.VMEM((4, MOM, w), BF),
            pltpu.VMEM((3, MOM, w), BF),
            pltpu.VMEM((4, 4, 2, MOM, w), BF),
            pltpu.VMEM((MOM, w), F32),
            pltpu.VMEM((MOM, w), F32),
        ]
    scratch += [pltpu.VMEM((256, w), BF) for w in WIDTHS]
    scratch += [pltpu.VMEM((T, 4, SUB, 128), jnp.int32)]
    any_space = pl.BlockSpec(memory_space=pl.ANY)
    return pl.pallas_call(
        kernel,
        out_shape=(
            jax.ShapeDtypeStruct((MOM, FF), F32),
            jax.ShapeDtypeStruct((MOM, FF), F32),
            jax.ShapeDtypeStruct((256, FF), BF),
        ),
        in_specs=[any_space] * 5 + [pl.BlockSpec(memory_space=pltpu.VMEM)],
        out_specs=(any_space,) * 3,
        scratch_shapes=scratch,
        compiler_params=pltpu.CompilerParams(
            collective_id=0, has_side_effects=True, vmem_limit_bytes=56 * 2**20
        ),
        cost_estimate=pl.CostEstimate(flops=2 * 10**9, bytes_accessed=4 * 10**6, transcendentals=0),
        name="galore",
    )(layer_input, out_grad, projector, first_moment, second_moment, doc_ids.reshape(1, TOK))


def solution(mesh):
    placed = (
        P("dp", "shard"),
        P("dp", "shard"),
        P(("dp", "shard"), None),
        P("dp", "shard"),
        P("dp", "shard"),
        P("dp"),
    )
    return jax.shard_map(
        local,
        mesh=mesh,
        in_specs=placed,
        out_specs=(P("dp", "shard"), P("dp", "shard"), P("dp", "shard")),
        check_vma=False,
    )
```

```python
import jax
import jax.numpy as jnp
from jax import lax
from jax.experimental import pallas as pl
from jax.experimental.pallas import tpu as pltpu
from jax.sharding import PartitionSpec as P

MESH = pl.DeviceIdType.MESH
BF = jnp.bfloat16
F32 = jnp.float32

beta_first = 0.9
beta_second = 0.95
bias_first = 1.0 - beta_first**2
bias_second = 1.0 - beta_second**2
epsilon = 1e-08

TOK, FEAT, RANK, FF, ROWS, MOM = 512, 512, 1024, 896, 16, 32
HALF = RANK // 2
QUARTER = RANK // 4
SUB = TOK // 16
PARTS = ((0, 0, 896), (1, 0, 384), (1, 384, 512))
N_PARTS = len(PARTS)
ORDER = (
    ("cnt", 0), ("hop", 0), ("cnt", 1), ("hop", 1), ("cnt", 2), ("zl", 0), ("zl", 1), ("y", 0), ("mm", 0),
    ("mm", 1), ("y", 1), ("mm", 3), ("mm", 2), ("sx", 0), ("sx", 1), ("sx", 3), ("sz", 0), ("sx", 2),
    ("sz", 1), ("sz", 3), ("gx", 0), ("sz", 2), ("gx", 1), ("turn", 0), ("gx", 3), ("fz",), ("gx", 2),
    ("turn", 1), ("mm2", 0), ("turn", 3), ("sc", 0), ("turn", 2), ("mm2", 2), ("mm2", 1), ("fx",), ("sc", 2),
    ("sc", 1), ("sy", 0), ("sy", 2), ("sy", 1), ("adam", 0), ("adam", 2), ("adam", 1), ("gy", 0), ("gy", 2),
    ("gy", 1), ("gc", 0), ("up", 0), ("gc", 2), ("gc", 1), ("up", 2), ("up", 1),
)
N_SEM = 31 + 6 * N_PARTS
N_FIXED = 21
N_EACH = 9


def kernel(x_hbm, g_hbm, p_hbm, m_hbm, v_hbm, ids_ref, m_out, v_out, u_out, *scratch):
    (
        x_in, g_in, m_in, v_in, p_in, rows_in, rows_up,
        part32, part, x_got, xsum32, xsum, z_got, wide, wide_t,
        count, count_got, u_sum,
        loc_sem, send_sem, recv_sem,
    ) = scratch[:N_FIXED]
    of_part = [scratch[N_FIXED + N_EACH * e : N_FIXED + N_EACH * (e + 1)] for e in range(N_PARTS)]
    m_new, v_new, u_new, weights = scratch[N_FIXED + N_EACH * N_PARTS :]

    d, s = lax.axis_index("dp"), lax.axis_index("shard")
    core = lax.rem(d, 2)
    zl = lax.rem(lax.div(d, 2), 4)
    y = lax.div(d, 8)
    x = lax.rem(s, 4)
    zh = lax.div(s, 4)

    def device(y=y, zl=zl, core=core, zh=zh, x=x):
        return ((y * 4 + zl) * 2 + core, zh * 4 + x)

    def up(value, k):
        return lax.rem(value + k, 4)

    other = 1 - core
    x_peers = [up(x, k) for k in (1, 3, 2)]
    y_peers = [up(y, k) for k in (1, 3, 2)]
    zl_peers = [up(zl, k) for k in (1, 3, 2)]
    zh_peers = [up(zh, k) for k in (1, 3, 2)]

    used = [0]
    flying = {}
    groups = []

    def send(name, whole, copies):
        i = used[0]
        used[0] += 1
        for src, dst, to in copies:
            pltpu.make_async_remote_copy(
                src_ref=src, dst_ref=dst, send_sem=send_sem.at[i], recv_sem=recv_sem.at[i],
                device_id=to, device_id_type=MESH,
            ).start()
        flying[name] = (whole, i)
        groups.append((whole, i))

    def arrive(name):
        whole, i = flying.pop(name)
        pltpu.make_async_copy(whole, whole, recv_sem.at[i]).wait()

    own_rows = pltpu.make_async_copy(p_hbm, p_in, loc_sem.at[0])
    loads = [
        pltpu.make_async_copy(x_hbm, x_in, loc_sem.at[1]),
        pltpu.make_async_copy(g_hbm, g_in, loc_sem.at[2]),
        pltpu.make_async_copy(m_hbm, m_in, loc_sem.at[3]),
        pltpu.make_async_copy(v_hbm, v_in, loc_sem.at[4]),
    ]
    own_rows.start()
    for cp in loads:
        cp.start()

    to_hop = device(y=up(zh, y), zl=x, zh=y, x=zl)
    seat = up(y, 4 - zh)
    from_hop = device(y=zh, zl=x, zh=seat, x=zl)
    moves = jnp.logical_or(x != zl, jnp.logical_or(y != 0, zh != 0))
    barrier = pltpu.get_barrier_semaphore()
    greet = [device(core=other)]
    greet += [device(x=p) for p in x_peers] + [device(y=p) for p in y_peers]
    greet += [device(zl=p) for p in zl_peers] + [device(zh=p) for p in zh_peers]
    for to in greet:
        pl.semaphore_signal(barrier, inc=1, device_id=to, device_id_type=MESH)

    @pl.when(moves)
    def _():
        pl.semaphore_signal(barrier, inc=1, device_id=from_hop, device_id_type=MESH)

    own_rows.wait()
    held = p_in[...].astype(F32)
    turned = [held] + [jnp.concatenate([held[:, k:], held[:, :k]], axis=1) for k in (32, 16, 48)]
    turned = jnp.concatenate(turned, axis=0).astype(BF)
    at = lax.broadcasted_iota(jnp.int32, (RANK, QUARTER), 0)
    col = lax.broadcasted_iota(jnp.int32, (1, QUARTER), 1)
    pick = (at == (col >> 4) * 64 + (col & 15)).astype(F32).astype(BF)
    moved = jnp.dot(turned, pick, preferred_element_type=F32).astype(BF)
    for r in range(4):
        h, c = divmod(r, 2)
        rows_up[h, zh, x, :, c * QUARTER : (c + 1) * QUARTER] = moved[r * ROWS : (r + 1) * ROWS]

    ids = jnp.transpose(jnp.broadcast_to(ids_ref[...], (128, TOK)))
    match = (ids == lax.broadcasted_iota(jnp.int32, (TOK, 128), 1)).astype(F32)
    count[0] = jnp.broadcast_to(jnp.sum(match, axis=0, keepdims=True), (8, 128))

    pl.semaphore_wait(barrier, len(greet) + moves.astype(jnp.int32))

    def hop(h):
        return pltpu.make_async_remote_copy(
            src_ref=rows_up.at[h, zh, x], dst_ref=rows_in.at[h, core, zh, x],
            send_sem=send_sem.at[N_SEM - 1 - h], recv_sem=recv_sem.at[N_SEM - 1 - h],
            device_id=to_hop, device_id_type=MESH,
        )

    @pl.when(moves)
    def _():
        hop(0).start()
        hop(1).start()

    send(("CNT", 0), count_got.at[0], [(count.at[0], count_got.at[0], device(core=other))])

    @pl.when(jnp.logical_not(moves))
    def _():
        for h in range(2):
            rows_in[h, core, zh, x] = rows_up[h, zh, x]

    def do_cnt(i):
        if i == 0:
            arrive(("CNT", 0))
            count[1] = count[0] + count_got[0]
            send(("cnt", 0), count_got.at[pl.ds(1, 3)], [
                (count.at[1], count_got.at[1 + k], device(zl=p)) for k, p in enumerate(zl_peers)
            ])
        elif i == 1:
            arrive(("cnt", 0))
            count[2] = count[1] + count_got[1] + count_got[2] + count_got[3]
            send(("cnt", 1), count_got.at[pl.ds(4, 3)], [
                (count.at[2], count_got.at[4 + k], device(y=p)) for k, p in enumerate(y_peers)
            ])
        else:
            arrive(("cnt", 1))
            lengths = count[2] + count_got[4] + count_got[5] + count_got[6]
            inverse = 1.0 / lengths[0:1]
            mine = ids_ref[:, pl.ds(pl.multiple_of(x * 128, 128), 128)]
            mine = jnp.transpose(jnp.broadcast_to(mine, (128, 128)))
            here = mine == lax.broadcasted_iota(jnp.int32, (128, 128), 1)
            weight = jnp.sum(jnp.where(here, inverse, 0.0), axis=1, keepdims=True)
            weights[...] = jnp.broadcast_to(weight, (128, 128)).reshape(4, SUB, 128)

    def do_hop(h):
        @pl.when(moves)
        def _():
            hop(h).wait_recv()

        mine = rows_in.at[h, core, seat, zl]
        send(("hop", h), rows_in.at[h, core, 0, pl.ds(0, 3)], [
            (mine, mine, device(zl=p)) for p in zl_peers
        ])

    def do_zl(h):
        arrive(("hop", h))
        mine = rows_in.at[h, core, seat]
        send(("zl", h), rows_in.at[h, core, pl.ds(0, 3)], [
            (mine, mine, device(y=p)) for p in y_peers
        ])

    def do_y(h):
        arrive(("zl", h))
        mine = rows_in.at[h, core]
        send(("y", h), mine, [(mine, mine, device(core=other))])

    def do_mm(r):
        h, c = divmod(r, 2)
        if ("y", h) in flying:
            arrive(("y", h))
        if loads:
            for cp in loads:
                cp.wait()
            loads.clear()
        rhs = rows_in[h].reshape(FEAT, HALF)[:, c * QUARTER : (c + 1) * QUARTER]
        value = jnp.dot(x_in[...], rhs, preferred_element_type=F32).reshape(4, 4, SUB, QUARTER)
        part32[r] = value
        part[r] = value.astype(BF)
        send(("mm", r), x_got.at[r], [
            (part.at[r, p], x_got.at[r, k], device(x=p)) for k, p in enumerate(x_peers)
        ])

    def do_sx(r):
        arrive(("mm", r))
        total = part32[r, x]
        for k in range(3):
            total = total + x_got[r, k].astype(F32)
        xsum32[r] = total
        xsum[r] = total.astype(BF)
        send(("sx", r), z_got.at[r], [
            (xsum.at[r, p], z_got.at[r, k], device(zh=p)) for k, p in enumerate(zh_peers)
        ])

    def do_sz(r):
        arrive(("sx", r))
        total = xsum32[r, zh]
        for k in range(3):
            total = total + z_got[r, k].astype(F32)
        wide[r, x, zh] = (total * weights[zh][:, 0:1]).astype(BF)
        mine = wide.at[r, x, zh]
        send(("sz", r), wide.at[r, x, pl.ds(0, 3)], [(mine, mine, device(zh=p)) for p in zh_peers])

    def do_gx(r):
        arrive(("sz", r))
        mine = wide.at[r, x]
        send(("gx", r), wide.at[r, pl.ds(0, 3)], [(mine, mine, device(x=p)) for p in x_peers])

    def do_turn(r):
        arrive(("gx", r))
        wide_t[r] = jnp.transpose(wide[r].reshape(TOK, QUARTER))

    def do_fz():
        mine = rows_up.at[:, zh, x]
        send(("fz",), rows_up.at[:, pl.ds(0, 3), x], [(mine, mine, device(zh=p)) for p in zh_peers])

    def do_fx():
        arrive(("fz",))
        mine = rows_up.at[:, :, x]
        send(("fx",), rows_up.at[:, :, pl.ds(0, 3)], [(mine, mine, device(x=p)) for p in x_peers])

    def do_mm2(e):
        h, start, width = PARTS[e]
        g_own, g_peer, c_got = of_part[e][0:3]
        cols = pl.ds(start, width)
        value = jnp.dot(wide_t[2 * h + other], g_in[:, cols], preferred_element_type=F32)
        g_peer[...] = value.astype(BF).reshape(4, 4, 16, width)
        send(("mm2", e), c_got, [(g_peer, c_got, device(core=other))])
        value = jnp.dot(wide_t[2 * h + core], g_in[:, cols], preferred_element_type=F32)
        g_own[...] = value.reshape(4, 4, 16, width)

    def do_sc(e):
        g_own, _, c_got, ysum, y_got = of_part[e][0:5]
        arrive(("mm2", e))
        for k, p in enumerate(y_peers):
            ysum[k] = (g_own[p] + c_got[p].astype(F32)).astype(BF)
        send(("sc", e), y_got, [
            (ysum.at[k], y_got.at[k], device(y=p)) for k, p in enumerate(y_peers)
        ])

    def do_sy(e):
        g_own, _, c_got, _, y_got, zsum32, zsum, l_got = of_part[e][0:8]
        total = g_own[y] + c_got[y].astype(F32)
        arrive(("sc", e))
        for k in range(3):
            total = total + y_got[k].astype(F32)
        zsum32[...] = total
        zsum[...] = total.astype(BF)
        send(("sy", e), l_got, [
            (zsum.at[p], l_got.at[k], device(zl=p)) for k, p in enumerate(zl_peers)
        ])

    def do_adam(e):
        h, start, width = PARTS[e]
        zsum32, _, l_got, full = of_part[e][5:9]
        rows, cols = pl.ds(h * 16, 16), pl.ds(start, width)
        arrive(("sy", e))
        grad = zsum32[zl]
        for k in range(3):
            grad = grad + l_got[k].astype(F32)
        first = beta_first * m_in[rows, cols] + (1.0 - beta_first) * grad
        second = beta_second * v_in[rows, cols] + (1.0 - beta_second) * (grad * grad)
        way = first / bias_first / (jnp.sqrt(second / bias_second) + epsilon)
        full[core, y, zl] = way.astype(BF)
        mine = full.at[core, y, zl]
        send(("adam", e), full.at[core, y, pl.ds(0, 3)], [
            (mine, mine, device(zl=p)) for p in zl_peers
        ])
        m_new[rows, cols] = first
        v_new[rows, cols] = second

    def do_gy(e):
        full = of_part[e][8]
        arrive(("adam", e))
        mine = full.at[core, y]
        send(("gy", e), full.at[core, pl.ds(0, 3)], [(mine, mine, device(y=p)) for p in y_peers])

    def do_gc(e):
        full = of_part[e][8]
        arrive(("gy", e))
        mine = full.at[core]
        send(("gc", e), mine, [(mine, mine, device(core=other))])

    def do_up(e):
        h, start, width = PARTS[e]
        full = of_part[e][8]
        if ("fx",) in flying:
            arrive(("fx",))
        arrive(("gc", e))
        lhs = rows_up[h].reshape(256, HALF)
        value = jnp.dot(lhs, full[...].reshape(HALF, width), preferred_element_type=F32)
        if h == 0:
            u_sum[:, pl.ds(start, width)] = value
        else:
            value = value + u_sum[:, pl.ds(start, width)]
            u_new[:, pl.ds(start, width)] = value.astype(BF)

    steps = {
        "hop": do_hop, "zl": do_zl, "y": do_y, "cnt": do_cnt, "mm": do_mm, "sx": do_sx,
        "sz": do_sz, "gx": do_gx, "turn": do_turn, "fz": do_fz, "fx": do_fx, "mm2": do_mm2,
        "sc": do_sc, "sy": do_sy, "adam": do_adam, "gy": do_gy, "gc": do_gc, "up": do_up,
    }
    for name, *which in ORDER:
        steps[name](*which)

    outs = [
        pltpu.make_async_copy(value, out, loc_sem.at[i])
        for i, (value, out) in enumerate(((m_new, m_out), (v_new, v_out), (u_new, u_out)))
    ]
    for cp in outs:
        cp.start()

    @pl.when(moves)
    def _():
        hop(0).wait_send()
        hop(1).wait_send()

    for whole, i in groups:
        pltpu.make_async_copy(whole, whole, send_sem.at[i]).wait()
    for cp in outs:
        cp.wait()


def hand_on(m_in, v_in, u_in, m_out, v_out, u_out, m_held, v_held, u_held, sem):
    ways = ((m_in, m_held, m_out), (v_in, v_held, v_out), (u_in, u_held, u_out))
    reads = [pltpu.make_async_copy(a, b, sem.at[i]) for i, (a, b, _) in enumerate(ways)]
    writes = [pltpu.make_async_copy(b, c, sem.at[3 + i]) for i, (_, b, c) in enumerate(ways)]
    for cp in reads:
        cp.start()
    for read, write in zip(reads, writes):
        read.wait()
        write.start()
    for cp in writes:
        cp.wait()


def local(layer_input, out_grad, projector, first_moment, second_moment, doc_ids):
    scratch = [
        pltpu.VMEM((TOK, FEAT), BF),
        pltpu.VMEM((TOK, FF), BF),
        pltpu.VMEM((MOM, FF), F32),
        pltpu.VMEM((MOM, FF), F32),
        pltpu.VMEM((ROWS, RANK), BF),
        pltpu.VMEM((2, 2, 4, 4, ROWS, HALF), BF),
        pltpu.VMEM((2, 4, 4, ROWS, HALF), BF),
        pltpu.VMEM((4, 4, 4, SUB, QUARTER), F32),
        pltpu.VMEM((4, 4, 4, SUB, QUARTER), BF),
        pltpu.VMEM((4, 3, 4, SUB, QUARTER), BF),
        pltpu.VMEM((4, 4, SUB, QUARTER), F32),
        pltpu.VMEM((4, 4, SUB, QUARTER), BF),
        pltpu.VMEM((4, 3, SUB, QUARTER), BF),
        pltpu.VMEM((4, 4, 4, SUB, QUARTER), BF),
        pltpu.VMEM((4, QUARTER, TOK), BF),
        pltpu.VMEM((3, 8, 128), F32),
        pltpu.VMEM((7, 8, 128), F32),
        pltpu.VMEM((256, FF), F32),
        pltpu.SemaphoreType.DMA((5,)),
        pltpu.SemaphoreType.DMA((N_SEM,)),
        pltpu.SemaphoreType.DMA((N_SEM,)),
    ]
    for _, _, w in PARTS:
        scratch += [
            pltpu.VMEM((4, 4, 16, w), F32),
            pltpu.VMEM((4, 4, 16, w), BF),
            pltpu.VMEM((4, 4, 16, w), BF),
            pltpu.VMEM((3, 4, 16, w), BF),
            pltpu.VMEM((3, 4, 16, w), BF),
            pltpu.VMEM((4, 16, w), F32),
            pltpu.VMEM((4, 16, w), BF),
            pltpu.VMEM((3, 16, w), BF),
            pltpu.VMEM((2, 4, 4, 16, w), BF),
        ]
    scratch += [
        pltpu.VMEM((MOM, FF), F32),
        pltpu.VMEM((MOM, FF), F32),
        pltpu.VMEM((256, FF), BF),
        pltpu.VMEM((4, SUB, 128), F32),
    ]
    any_space = pl.BlockSpec(memory_space=pl.ANY)
    results = (
        jax.ShapeDtypeStruct((MOM, FF), F32),
        jax.ShapeDtypeStruct((MOM, FF), F32),
        jax.ShapeDtypeStruct((256, FF), BF),
    )
    made = pl.pallas_call(
        kernel,
        out_shape=results,
        in_specs=[any_space] * 5 + [pl.BlockSpec(memory_space=pltpu.VMEM)],
        out_specs=(any_space,) * 3,
        scratch_shapes=scratch,
        compiler_params=pltpu.CompilerParams(
            collective_id=0, has_side_effects=True, vmem_limit_bytes=56 * 2**20
        ),
        cost_estimate=pl.CostEstimate(flops=2 * 10**9, bytes_accessed=4 * 10**6, transcendentals=0),
        name="galore",
    )(layer_input, out_grad, projector, first_moment, second_moment, doc_ids.reshape(1, TOK))
    return pl.pallas_call(
        hand_on,
        out_shape=results,
        in_specs=[any_space] * 3,
        out_specs=(any_space,) * 3,
        scratch_shapes=[
            pltpu.VMEM((MOM, FF), F32),
            pltpu.VMEM((MOM, FF), F32),
            pltpu.VMEM((256, FF), BF),
            pltpu.SemaphoreType.DMA((6,)),
        ],
        compiler_params=pltpu.CompilerParams(vmem_limit_bytes=56 * 2**20),
        name="hand_on",
    )(*made)


def solution(mesh):
    placed = (
        P("dp", "shard"),
        P("dp", "shard"),
        P(("dp", "shard"), None),
        P("dp", "shard"),
        P("dp", "shard"),
        P("dp"),
    )
    return jax.shard_map(
        local,
        mesh=mesh,
        in_specs=placed,
        out_specs=(P("dp", "shard"), P("dp", "shard"), P("dp", "shard")),
        check_vma=False,
    )
```

```python
import jax
import jax.numpy as jnp
from jax import lax
from jax.experimental import pallas as pl
from jax.experimental.pallas import tpu as pltpu
from jax.sharding import PartitionSpec as P

MESH = pl.DeviceIdType.MESH
BF = jnp.bfloat16
F32 = jnp.float32

beta_first = 0.9
beta_second = 0.95
bias_first = 1.0 - beta_first**2
bias_second = 1.0 - beta_second**2
epsilon = 1e-08

TOK, FEAT, RANK, FF, ROWS, MOM = 512, 512, 1024, 896, 16, 32
HALF = RANK // 2
QUARTER = RANK // 4
SUB = TOK // 16
PARTS = ((0, 0, 896), (1, 0, 384), (1, 384, 512))
N_PARTS = len(PARTS)
ORDER = (
    ("cnt", 0), ("hop", 0), ("cnt", 1), ("hop", 1), ("cnt", 2), ("zl", 0), ("fz",), ("zl", 1), ("mm", 1),
    ("mm", 0), ("mm", 3), ("mm", 2), ("sx", 1), ("sx", 0), ("sx", 3), ("sz", 1), ("sx", 2), ("sz", 0),
    ("sz", 3), ("fx",), ("gx", 1), ("sz", 2), ("gx", 0), ("gx", 3), ("turn", 1), ("gx", 2), ("turn", 0),
    ("mm2", 0), ("turn", 3), ("turn", 2), ("mm2", 2), ("mm2", 1), ("sy", 0), ("sy", 2), ("adam", 0),
    ("sy", 1), ("adam", 2), ("gy", 0), ("adam", 1), ("gy", 2), ("gy", 1), ("gc", 0), ("up", 0), ("gc", 2),
    ("gc", 1), ("up", 2), ("up", 1),
)
N_SEM = 34 + 5 * N_PARTS
N_FIXED = 22
N_EACH = 7


def kernel(x_hbm, g_hbm, p_hbm, m_hbm, v_hbm, ids_ref, m_out, v_out, u_out, *scratch):
    (
        x_in, g_in, m_in, v_in, p_in, rows_in, rows_up,
        part32, part, x_got, xsum32, xsum, z_got, wide, wide_t,
        count, count_got, ids_all, u_sum,
        loc_sem, send_sem, recv_sem,
    ) = scratch[:N_FIXED]
    of_part = [scratch[N_FIXED + N_EACH * e : N_FIXED + N_EACH * (e + 1)] for e in range(N_PARTS)]
    m_new, v_new, u_new, weights = scratch[N_FIXED + N_EACH * N_PARTS :]

    d, s = lax.axis_index("dp"), lax.axis_index("shard")
    core = lax.rem(d, 2)
    zl = lax.rem(lax.div(d, 2), 4)
    y = lax.div(d, 8)
    x = lax.rem(s, 4)
    zh = lax.div(s, 4)

    def device(y=y, zl=zl, core=core, zh=zh, x=x):
        return ((y * 4 + zl) * 2 + core, zh * 4 + x)

    def up(value, k):
        return lax.rem(value + k, 4)

    other = 1 - core
    x_peers = [up(x, k) for k in (1, 3, 2)]
    y_peers = [up(y, k) for k in (1, 3, 2)]
    zl_peers = [up(zl, k) for k in (1, 3, 2)]
    zh_peers = [up(zh, k) for k in (1, 3, 2)]

    used = [0]
    flying = {}
    groups = []

    def send(name, whole, copies):
        i = used[0]
        used[0] += 1
        for src, dst, to in copies:
            pltpu.make_async_remote_copy(
                src_ref=src, dst_ref=dst, send_sem=send_sem.at[i], recv_sem=recv_sem.at[i],
                device_id=to, device_id_type=MESH,
            ).start()
        flying[name] = (whole, i)
        groups.append((whole, i))

    def arrive(name):
        whole, i = flying.pop(name)
        pltpu.make_async_copy(whole, whole, recv_sem.at[i]).wait()

    own_rows = pltpu.make_async_copy(p_hbm, p_in, loc_sem.at[0])
    loads = [
        pltpu.make_async_copy(x_hbm, x_in.at[core], loc_sem.at[1]),
        pltpu.make_async_copy(g_hbm, g_in.at[core], loc_sem.at[2]),
        pltpu.make_async_copy(m_hbm, m_in, loc_sem.at[3]),
        pltpu.make_async_copy(v_hbm, v_in, loc_sem.at[4]),
    ]
    own_rows.start()
    for cp in loads:
        cp.start()

    to_hop = [device(y=up(zh, y), zl=x, zh=y, x=zl, core=c) for c in range(2)]
    seat = up(y, 4 - zh)
    from_hop = [device(y=zh, zl=x, zh=seat, x=zl, core=c) for c in range(2)]
    moves = jnp.logical_or(x != zl, jnp.logical_or(y != 0, zh != 0))
    barrier = pltpu.get_barrier_semaphore()
    greet = [device(core=other)]
    greet += [device(x=p) for p in x_peers] + [device(y=p) for p in y_peers]
    greet += [device(zl=p) for p in zl_peers] + [device(zh=p) for p in zh_peers]
    for to in greet:
        pl.semaphore_signal(barrier, inc=1, device_id=to, device_id_type=MESH)

    @pl.when(moves)
    def _():
        for to in from_hop:
            pl.semaphore_signal(barrier, inc=1, device_id=to, device_id_type=MESH)

    own_rows.wait()
    held = p_in[...].astype(F32)
    turned = [held] + [jnp.concatenate([held[:, k:], held[:, :k]], axis=1) for k in (32, 16, 48)]
    turned = jnp.concatenate(turned, axis=0).astype(BF)
    at = lax.broadcasted_iota(jnp.int32, (RANK, QUARTER), 0)
    col = lax.broadcasted_iota(jnp.int32, (1, QUARTER), 1)
    pick = (at == (col >> 4) * 64 + (col & 15)).astype(F32).astype(BF)
    moved = jnp.dot(turned, pick, preferred_element_type=F32).astype(BF)
    for r in range(4):
        h, c = divmod(r, 2)
        rows_up[h, c, zh, x] = moved[r * ROWS : (r + 1) * ROWS]

    ids = jnp.transpose(jnp.broadcast_to(ids_ref[...], (128, TOK)))
    match = (ids == lax.broadcasted_iota(jnp.int32, (TOK, 128), 1)).astype(F32)
    count[0] = jnp.broadcast_to(jnp.sum(match, axis=0, keepdims=True), (8, 128))

    pl.semaphore_wait(barrier, len(greet) + 2 * moves.astype(jnp.int32))

    def hop(h, c):
        i = N_SEM - 1 - (2 * h + c)
        return pltpu.make_async_remote_copy(
            src_ref=rows_up.at[h, c, zh, x], dst_ref=rows_in.at[h, core, zh, x],
            send_sem=send_sem.at[i], recv_sem=recv_sem.at[N_SEM - 1 - (2 * h + core)],
            device_id=to_hop[c], device_id_type=MESH,
        )

    def stay(h):
        return pltpu.make_async_remote_copy(
            src_ref=rows_up.at[h, other, zh, x], dst_ref=rows_in.at[h, core, zh, x],
            send_sem=send_sem.at[N_SEM - 1 - (2 * h + other)],
            recv_sem=recv_sem.at[N_SEM - 1 - (2 * h + core)],
            device_id=device(core=other), device_id_type=MESH,
        )

    def hop_wait(h, c, sems):
        whole = rows_up.at[h, c, zh, x]
        pltpu.make_async_copy(whole, whole, sems.at[N_SEM - 1 - (2 * h + c)]).wait()

    @pl.when(moves)
    def _():
        for h in range(2):
            for c in range(2):
                hop(h, c).start()

    @pl.when(jnp.logical_not(moves))
    def _():
        for h in range(2):
            stay(h).start()
            rows_in[h, core, zh, x] = rows_up[h, core, zh, x]

    for cp in loads[:2]:
        cp.wait()
    to = device(core=other)
    ids_all[core] = ids_ref[...]
    send(("CNT", 0), count_got.at[0], [(count.at[0], count_got.at[0], to)])
    send(("ids",), ids_all.at[0], [(ids_all.at[core], ids_all.at[core], to)])
    send(("xin",), x_in.at[0], [(x_in.at[core], x_in.at[core], to)])
    send(("gin",), g_in.at[0], [(g_in.at[core], g_in.at[core], to)])

    def do_cnt(i):
        if i == 0:
            arrive(("CNT", 0))
            count[1] = count[0] + count_got[0]
            send(("cnt", 0), count_got.at[pl.ds(1, 3)], [
                (count.at[1], count_got.at[1 + k], device(zl=p)) for k, p in enumerate(zl_peers)
            ])
        elif i == 1:
            arrive(("cnt", 0))
            count[2] = count[1] + count_got[1] + count_got[2] + count_got[3]
            send(("cnt", 1), count_got.at[pl.ds(4, 3)], [
                (count.at[2], count_got.at[4 + k], device(y=p)) for k, p in enumerate(y_peers)
            ])
        else:
            arrive(("cnt", 1))
            lengths = count[2] + count_got[4] + count_got[5] + count_got[6]
            inverse = 1.0 / lengths[0:1]
            arrive(("ids",))
            for b in range(2):
                mine = ids_all[b, :, pl.ds(pl.multiple_of(x * 128, 128), 128)]
                mine = jnp.transpose(jnp.broadcast_to(mine, (128, 128)))
                here = mine == lax.broadcasted_iota(jnp.int32, (128, 128), 1)
                weight = jnp.sum(jnp.where(here, inverse, 0.0), axis=1, keepdims=True)
                weights[b] = jnp.broadcast_to(weight, (128, 128)).reshape(4, SUB, 128)

    def do_hop(h):
        @pl.when(moves)
        def _():
            for c in range(2):
                hop_wait(h, c, recv_sem)

        @pl.when(jnp.logical_not(moves))
        def _():
            hop_wait(h, other, recv_sem)

        mine = rows_in.at[h, :, seat, zl]
        send(("hop", h), rows_in.at[h, :, 0, pl.ds(0, 3)], [
            (mine, mine, device(zl=p)) for p in zl_peers
        ])

    def do_zl(h):
        arrive(("hop", h))
        mine = rows_in.at[h, :, seat]
        send(("zl", h), rows_in.at[h, :, pl.ds(0, 3)], [
            (mine, mine, device(y=p)) for p in y_peers
        ])

    def do_mm(r):
        h, b = divmod(r, 2)
        for name in (("zl", h), ("xin",)):
            if name in flying:
                arrive(name)
        rhs = rows_in[h].reshape(FEAT, QUARTER)
        value = jnp.dot(x_in[b], rhs, preferred_element_type=F32).reshape(4, 4, SUB, QUARTER)
        part32[r] = value
        part[r] = value.astype(BF)
        send(("mm", r), x_got.at[r], [
            (part.at[r, p], x_got.at[r, k], device(x=p)) for k, p in enumerate(x_peers)
        ])

    def do_sx(r):
        arrive(("mm", r))
        total = part32[r, x]
        for k in range(3):
            total = total + x_got[r, k].astype(F32)
        xsum32[r] = total
        xsum[r] = total.astype(BF)
        send(("sx", r), z_got.at[r], [
            (xsum.at[r, p], z_got.at[r, k], device(zh=p)) for k, p in enumerate(zh_peers)
        ])

    def do_sz(r):
        arrive(("sx", r))
        total = xsum32[r, zh]
        for k in range(3):
            total = total + z_got[r, k].astype(F32)
        wide[r, x, zh] = (total * weights[r % 2, zh][:, 0:1]).astype(BF)
        mine = wide.at[r, x, zh]
        send(("sz", r), wide.at[r, x, pl.ds(0, 3)], [(mine, mine, device(zh=p)) for p in zh_peers])

    def do_gx(r):
        arrive(("sz", r))
        mine = wide.at[r, x]
        send(("gx", r), wide.at[r, pl.ds(0, 3)], [(mine, mine, device(x=p)) for p in x_peers])

    def do_turn(r):
        arrive(("gx", r))
        h, b = divmod(r, 2)
        wide_t[h, :, b * TOK : (b + 1) * TOK] = jnp.transpose(wide[r].reshape(TOK, QUARTER))

    def do_fz():
        mine = rows_up.at[:, :, zh, x]
        send(("fz",), rows_up.at[:, :, pl.ds(0, 3), x], [
            (mine, mine, device(zh=p)) for p in zh_peers
        ])

    def do_fx():
        arrive(("fz",))
        mine = rows_up.at[:, :, :, x]
        send(("fx",), rows_up.at[:, :, :, pl.ds(0, 3)], [(mine, mine, device(x=p)) for p in x_peers])

    def do_mm2(e):
        h, start, width = PARTS[e]
        g_own, ysum, y_got = of_part[e][0:3]
        if ("gin",) in flying:
            arrive(("gin",))
        rhs = g_in[...].reshape(2 * TOK, FF)[:, start : start + width]
        value = jnp.dot(wide_t[h], rhs, preferred_element_type=F32)
        g_own[...] = value.reshape(4, 4, 16, width)
        for k, p in enumerate(y_peers):
            ysum[k] = g_own[p].astype(BF)
        send(("mm2", e), y_got, [
            (ysum.at[k], y_got.at[k], device(y=p)) for k, p in enumerate(y_peers)
        ])

    def do_sy(e):
        g_own, _, y_got, zsum32, zsum, l_got = of_part[e][0:6]
        total = g_own[y]
        arrive(("mm2", e))
        for k in range(3):
            total = total + y_got[k].astype(F32)
        zsum32[...] = total
        zsum[...] = total.astype(BF)
        send(("sy", e), l_got, [
            (zsum.at[p], l_got.at[k], device(zl=p)) for k, p in enumerate(zl_peers)
        ])

    def do_adam(e):
        h, start, width = PARTS[e]
        zsum32, _, l_got, full = of_part[e][3:7]
        rows, cols = pl.ds(h * 16, 16), pl.ds(start, width)
        arrive(("sy", e))
        grad = zsum32[zl]
        for k in range(3):
            grad = grad + l_got[k].astype(F32)
        for cp in loads[2:]:
            cp.wait()
        del loads[2:]
        first = beta_first * m_in[rows, cols] + (1.0 - beta_first) * grad
        second = beta_second * v_in[rows, cols] + (1.0 - beta_second) * (grad * grad)
        way = first / bias_first / (jnp.sqrt(second / bias_second) + epsilon)
        full[core, y, zl] = way.astype(BF)
        mine = full.at[core, y, zl]
        send(("adam", e), full.at[core, y, pl.ds(0, 3)], [
            (mine, mine, device(zl=p)) for p in zl_peers
        ])
        m_new[rows, cols] = first
        v_new[rows, cols] = second

    def do_gy(e):
        full = of_part[e][6]
        arrive(("adam", e))
        mine = full.at[core, y]
        send(("gy", e), full.at[core, pl.ds(0, 3)], [(mine, mine, device(y=p)) for p in y_peers])

    def do_gc(e):
        full = of_part[e][6]
        arrive(("gy", e))
        mine = full.at[core]
        send(("gc", e), mine, [(mine, mine, device(core=other))])

    def do_up(e):
        h, start, width = PARTS[e]
        full = of_part[e][6]
        if ("fx",) in flying:
            arrive(("fx",))
        value = jnp.dot(
            rows_up[h, core].reshape(256, QUARTER), full[core].reshape(QUARTER, width),
            preferred_element_type=F32,
        )
        arrive(("gc", e))
        value = value + jnp.dot(
            rows_up[h, other].reshape(256, QUARTER), full[other].reshape(QUARTER, width),
            preferred_element_type=F32,
        )
        if h == 0:
            u_sum[:, pl.ds(start, width)] = value
        else:
            value = value + u_sum[:, pl.ds(start, width)]
            u_new[:, pl.ds(start, width)] = value.astype(BF)

    steps = {
        "hop": do_hop, "zl": do_zl, "cnt": do_cnt, "mm": do_mm, "sx": do_sx,
        "sz": do_sz, "gx": do_gx, "turn": do_turn, "fz": do_fz, "fx": do_fx, "mm2": do_mm2,
        "sy": do_sy, "adam": do_adam, "gy": do_gy, "gc": do_gc, "up": do_up,
    }
    for name, *which in ORDER:
        steps[name](*which)

    outs = [
        pltpu.make_async_copy(value, out, loc_sem.at[i])
        for i, (value, out) in enumerate(((m_new, m_out), (v_new, v_out), (u_new, u_out)))
    ]
    for cp in outs:
        cp.start()

    @pl.when(moves)
    def _():
        for h in range(2):
            for c in range(2):
                hop_wait(h, c, send_sem)

    @pl.when(jnp.logical_not(moves))
    def _():
        for h in range(2):
            hop_wait(h, other, send_sem)

    for whole, i in groups:
        pltpu.make_async_copy(whole, whole, send_sem.at[i]).wait()
    for cp in outs:
        cp.wait()


def hand_on(m_in, v_in, u_in, m_out, v_out, u_out, m_held, v_held, u_held, sem):
    ways = ((m_in, m_held, m_out), (v_in, v_held, v_out), (u_in, u_held, u_out))
    reads = [pltpu.make_async_copy(a, b, sem.at[i]) for i, (a, b, _) in enumerate(ways)]
    writes = [pltpu.make_async_copy(b, c, sem.at[3 + i]) for i, (_, b, c) in enumerate(ways)]
    for cp in reads:
        cp.start()
    for read, write in zip(reads, writes):
        read.wait()
        write.start()
    for cp in writes:
        cp.wait()


def local(layer_input, out_grad, projector, first_moment, second_moment, doc_ids):
    scratch = [
        pltpu.VMEM((2, TOK, FEAT), BF),
        pltpu.VMEM((2, TOK, FF), BF),
        pltpu.VMEM((MOM, FF), F32),
        pltpu.VMEM((MOM, FF), F32),
        pltpu.VMEM((ROWS, RANK), BF),
        pltpu.VMEM((2, 2, 4, 4, ROWS, QUARTER), BF),
        pltpu.VMEM((2, 2, 4, 4, ROWS, QUARTER), BF),
        pltpu.VMEM((4, 4, 4, SUB, QUARTER), F32),
        pltpu.VMEM((4, 4, 4, SUB, QUARTER), BF),
        pltpu.VMEM((4, 3, 4, SUB, QUARTER), BF),
        pltpu.VMEM((4, 4, SUB, QUARTER), F32),
        pltpu.VMEM((4, 4, SUB, QUARTER), BF),
        pltpu.VMEM((4, 3, SUB, QUARTER), BF),
        pltpu.VMEM((4, 4, 4, SUB, QUARTER), BF),
        pltpu.VMEM((2, QUARTER, 2 * TOK), BF),
        pltpu.VMEM((3, 8, 128), F32),
        pltpu.VMEM((7, 8, 128), F32),
        pltpu.VMEM((2, 1, TOK), jnp.int32),
        pltpu.VMEM((256, FF), F32),
        pltpu.SemaphoreType.DMA((5,)),
        pltpu.SemaphoreType.DMA((N_SEM,)),
        pltpu.SemaphoreType.DMA((N_SEM,)),
    ]
    for _, _, w in PARTS:
        scratch += [
            pltpu.VMEM((4, 4, 16, w), F32),
            pltpu.VMEM((3, 4, 16, w), BF),
            pltpu.VMEM((3, 4, 16, w), BF),
            pltpu.VMEM((4, 16, w), F32),
            pltpu.VMEM((4, 16, w), BF),
            pltpu.VMEM((3, 16, w), BF),
            pltpu.VMEM((2, 4, 4, 16, w), BF),
        ]
    scratch += [
        pltpu.VMEM((MOM, FF), F32),
        pltpu.VMEM((MOM, FF), F32),
        pltpu.VMEM((256, FF), BF),
        pltpu.VMEM((2, 4, SUB, 128), F32),
    ]
    any_space = pl.BlockSpec(memory_space=pl.ANY)
    results = (
        jax.ShapeDtypeStruct((MOM, FF), F32),
        jax.ShapeDtypeStruct((MOM, FF), F32),
        jax.ShapeDtypeStruct((256, FF), BF),
    )
    made = pl.pallas_call(
        kernel,
        out_shape=results,
        in_specs=[any_space] * 5 + [pl.BlockSpec(memory_space=pltpu.VMEM)],
        out_specs=(any_space,) * 3,
        scratch_shapes=scratch,
        compiler_params=pltpu.CompilerParams(
            collective_id=0, has_side_effects=True, vmem_limit_bytes=56 * 2**20
        ),
        cost_estimate=pl.CostEstimate(flops=2 * 10**9, bytes_accessed=4 * 10**6, transcendentals=0),
        name="galore",
    )(layer_input, out_grad, projector, first_moment, second_moment, doc_ids.reshape(1, TOK))
    return pl.pallas_call(
        hand_on,
        out_shape=results,
        in_specs=[any_space] * 3,
        out_specs=(any_space,) * 3,
        scratch_shapes=[
            pltpu.VMEM((MOM, FF), F32),
            pltpu.VMEM((MOM, FF), F32),
            pltpu.VMEM((256, FF), BF),
            pltpu.SemaphoreType.DMA((6,)),
        ],
        compiler_params=pltpu.CompilerParams(vmem_limit_bytes=56 * 2**20),
        name="hand_on",
    )(*made)


def solution(mesh):
    placed = (
        P("dp", "shard"),
        P("dp", "shard"),
        P(("dp", "shard"), None),
        P("dp", "shard"),
        P("dp", "shard"),
        P("dp"),
    )
    return jax.shard_map(
        local,
        mesh=mesh,
        in_specs=placed,
        out_specs=(P("dp", "shard"), P("dp", "shard"), P("dp", "shard")),
        check_vma=False,
    )
```

```python
import jax
import jax.numpy as jnp
from jax import lax
from jax.experimental import pallas as pl
from jax.experimental.pallas import tpu as pltpu
from jax.sharding import PartitionSpec as P

MESH = pl.DeviceIdType.MESH
BF = jnp.bfloat16
F32 = jnp.float32

beta_first = 0.9
beta_second = 0.95
bias_first = 1.0 - beta_first**2
bias_second = 1.0 - beta_second**2
epsilon = 1e-08

TOK, FEAT, RANK, FF, ROWS, MOM = 512, 512, 1024, 896, 16, 32
HALF = RANK // 2
QUARTER = RANK // 4
SUB = TOK // 16
PARTS = ((0, 0, 896), (1, 0, 384), (1, 384, 512))
N_PARTS = len(PARTS)
ORDER = (
    ("cnt", 0), ("hop", 0), ("cnt", 1), ("hop", 1), ("cnt", 2), ("zl", 0), ("zl", 1), ("mm", 1), ("mm", 0),
    ("mm", 3), ("mm", 2), ("sx", 1), ("sx", 0), ("sx", 3), ("sz", 1), ("sx", 2), ("sz", 0), ("sz", 3),
    ("gx", 1), ("sz", 2), ("gx", 0), ("gx", 3), ("turn", 1), ("gx", 2), ("fz",), ("turn", 0), ("mm2", 0),
    ("turn", 3), ("turn", 2), ("mm2", 2), ("mm2", 1), ("fx",), ("sy", 0), ("sy", 2), ("adam", 0), ("sy", 1),
    ("adam", 2), ("gy", 0), ("adam", 1), ("gy", 2), ("gy", 1), ("gc", 0), ("up", 0), ("gc", 2), ("gc", 1),
    ("up", 2), ("up", 1),
)
N_SEM = 34 + 5 * N_PARTS
N_FIXED = 22
N_EACH = 7


def kernel(x_hbm, g_hbm, p_hbm, m_hbm, v_hbm, ids_ref, m_out, v_out, u_out, *scratch):
    (
        x_in, g_in, m_in, v_in, p_in, rows_in, rows_up,
        part32, part, x_got, xsum32, xsum, z_got, wide, wide_t,
        count, count_got, ids_all, u_sum,
        loc_sem, send_sem, recv_sem,
    ) = scratch[:N_FIXED]
    of_part = [scratch[N_FIXED + N_EACH * e : N_FIXED + N_EACH * (e + 1)] for e in range(N_PARTS)]
    m_new, v_new, u_new, weights = scratch[N_FIXED + N_EACH * N_PARTS :]

    d, s = lax.axis_index("dp"), lax.axis_index("shard")
    core = lax.rem(d, 2)
    zl = lax.rem(lax.div(d, 2), 4)
    y = lax.div(d, 8)
    x = lax.rem(s, 4)
    zh = lax.div(s, 4)

    def device(y=y, zl=zl, core=core, zh=zh, x=x):
        return ((y * 4 + zl) * 2 + core, zh * 4 + x)

    def up(value, k):
        return lax.rem(value + k, 4)

    other = 1 - core
    x_peers = [up(x, k) for k in (2, 1, 3)]
    y_peers = [up(y, k) for k in (2, 1, 3)]
    zl_peers = [up(zl, k) for k in (2, 1, 3)]
    zh_peers = [up(zh, k) for k in (2, 1, 3)]

    used = [0]
    flying = {}
    groups = []

    def send(name, whole, copies):
        i = used[0]
        used[0] += 1
        for src, dst, to in copies:
            pltpu.make_async_remote_copy(
                src_ref=src, dst_ref=dst, send_sem=send_sem.at[i], recv_sem=recv_sem.at[i],
                device_id=to, device_id_type=MESH,
            ).start()
        flying[name] = (whole, i)
        groups.append((whole, i))

    def arrive(name):
        whole, i = flying.pop(name)
        pltpu.make_async_copy(whole, whole, recv_sem.at[i]).wait()

    own_rows = pltpu.make_async_copy(p_hbm, p_in, loc_sem.at[0])
    loads = [
        pltpu.make_async_copy(x_hbm, x_in.at[core], loc_sem.at[1]),
        pltpu.make_async_copy(g_hbm, g_in.at[core], loc_sem.at[2]),
        pltpu.make_async_copy(m_hbm, m_in, loc_sem.at[3]),
        pltpu.make_async_copy(v_hbm, v_in, loc_sem.at[4]),
    ]
    own_rows.start()
    for cp in loads:
        cp.start()

    to_hop = [device(y=up(zh, y), zl=x, zh=y, x=zl, core=c) for c in range(2)]
    seat = up(y, 4 - zh)
    from_hop = [device(y=zh, zl=x, zh=seat, x=zl, core=c) for c in range(2)]
    moves = jnp.logical_or(x != zl, jnp.logical_or(y != 0, zh != 0))
    barrier = pltpu.get_barrier_semaphore()
    greet = [device(core=other)]
    greet += [device(x=p) for p in x_peers] + [device(y=p) for p in y_peers]
    greet += [device(zl=p) for p in zl_peers] + [device(zh=p) for p in zh_peers]
    for to in greet:
        pl.semaphore_signal(barrier, inc=1, device_id=to, device_id_type=MESH)

    @pl.when(moves)
    def _():
        for to in from_hop:
            pl.semaphore_signal(barrier, inc=1, device_id=to, device_id_type=MESH)

    own_rows.wait()
    held = p_in[...].astype(F32)
    turned = [held] + [jnp.concatenate([held[:, k:], held[:, :k]], axis=1) for k in (32, 16, 48)]
    turned = jnp.concatenate(turned, axis=0).astype(BF)
    at = lax.broadcasted_iota(jnp.int32, (RANK, QUARTER), 0)
    col = lax.broadcasted_iota(jnp.int32, (1, QUARTER), 1)
    pick = (at == (col >> 4) * 64 + (col & 15)).astype(F32).astype(BF)
    moved = jnp.dot(turned, pick, preferred_element_type=F32).astype(BF)
    for r in range(4):
        h, c = divmod(r, 2)
        rows_up[h, c, zh, x] = moved[r * ROWS : (r + 1) * ROWS]

    ids = jnp.transpose(jnp.broadcast_to(ids_ref[...], (128, TOK)))
    match = (ids == lax.broadcasted_iota(jnp.int32, (TOK, 128), 1)).astype(F32)
    count[0] = jnp.broadcast_to(jnp.sum(match, axis=0, keepdims=True), (8, 128))

    pl.semaphore_wait(barrier, len(greet) + 2 * moves.astype(jnp.int32))

    def hop(h, c):
        i = N_SEM - 1 - (2 * h + c)
        return pltpu.make_async_remote_copy(
            src_ref=rows_up.at[h, c, zh, x], dst_ref=rows_in.at[h, core, zh, x],
            send_sem=send_sem.at[i], recv_sem=recv_sem.at[N_SEM - 1 - (2 * h + core)],
            device_id=to_hop[c], device_id_type=MESH,
        )

    def stay(h):
        return pltpu.make_async_remote_copy(
            src_ref=rows_up.at[h, other, zh, x], dst_ref=rows_in.at[h, core, zh, x],
            send_sem=send_sem.at[N_SEM - 1 - (2 * h + other)],
            recv_sem=recv_sem.at[N_SEM - 1 - (2 * h + core)],
            device_id=device(core=other), device_id_type=MESH,
        )

    def hop_wait(h, c, sems):
        whole = rows_up.at[h, c, zh, x]
        pltpu.make_async_copy(whole, whole, sems.at[N_SEM - 1 - (2 * h + c)]).wait()

    @pl.when(moves)
    def _():
        for h in range(2):
            for c in range(2):
                hop(h, c).start()

    @pl.when(jnp.logical_not(moves))
    def _():
        for h in range(2):
            stay(h).start()
            rows_in[h, core, zh, x] = rows_up[h, core, zh, x]

    for cp in loads[:2]:
        cp.wait()
    to = device(core=other)
    ids_all[core] = ids_ref[...]
    send(("CNT", 0), count_got.at[0], [(count.at[0], count_got.at[0], to)])
    send(("ids",), ids_all.at[0], [(ids_all.at[core], ids_all.at[core], to)])
    send(("xin",), x_in.at[0], [(x_in.at[core], x_in.at[core], to)])
    send(("gin",), g_in.at[0], [(g_in.at[core], g_in.at[core], to)])

    def do_cnt(i):
        if i == 0:
            arrive(("CNT", 0))
            count[1] = count[0] + count_got[0]
            send(("cnt", 0), count_got.at[pl.ds(1, 3)], [
                (count.at[1], count_got.at[1 + k], device(zl=p)) for k, p in enumerate(zl_peers)
            ])
        elif i == 1:
            arrive(("cnt", 0))
            count[2] = count[1] + count_got[1] + count_got[2] + count_got[3]
            send(("cnt", 1), count_got.at[pl.ds(4, 3)], [
                (count.at[2], count_got.at[4 + k], device(y=p)) for k, p in enumerate(y_peers)
            ])
        else:
            arrive(("cnt", 1))
            lengths = count[2] + count_got[4] + count_got[5] + count_got[6]
            inverse = 1.0 / lengths[0:1]
            arrive(("ids",))
            for b in range(2):
                mine = ids_all[b, :, pl.ds(pl.multiple_of(x * 128, 128), 128)]
                mine = jnp.transpose(jnp.broadcast_to(mine, (128, 128)))
                here = mine == lax.broadcasted_iota(jnp.int32, (128, 128), 1)
                weight = jnp.sum(jnp.where(here, inverse, 0.0), axis=1, keepdims=True)
                weights[b] = jnp.broadcast_to(weight, (128, 128)).reshape(4, SUB, 128)

    def do_hop(h):
        @pl.when(moves)
        def _():
            for c in range(2):
                hop_wait(h, c, recv_sem)

        @pl.when(jnp.logical_not(moves))
        def _():
            hop_wait(h, other, recv_sem)

        mine = rows_in.at[h, :, seat, zl]
        send(("hop", h), rows_in.at[h, :, 0, pl.ds(0, 3)], [
            (mine, mine, device(zl=p)) for p in zl_peers
        ])

    def do_zl(h):
        arrive(("hop", h))
        mine = rows_in.at[h, :, seat]
        send(("zl", h), rows_in.at[h, :, pl.ds(0, 3)], [
            (mine, mine, device(y=p)) for p in y_peers
        ])

    def do_mm(r):
        h, b = divmod(r, 2)
        for name in (("zl", h), ("xin",)):
            if name in flying:
                arrive(name)
        rhs = rows_in[h].reshape(FEAT, QUARTER)
        value = jnp.dot(x_in[b], rhs, preferred_element_type=F32).reshape(4, 4, SUB, QUARTER)
        part32[r] = value
        part[r] = value.astype(BF)
        send(("mm", r), x_got.at[r], [
            (part.at[r, p], x_got.at[r, k], device(x=p)) for k, p in enumerate(x_peers)
        ])

    def do_sx(r):
        arrive(("mm", r))
        total = part32[r, x]
        for k in range(3):
            total = total + x_got[r, k].astype(F32)
        xsum32[r] = total
        xsum[r] = total.astype(BF)
        send(("sx", r), z_got.at[r], [
            (xsum.at[r, p], z_got.at[r, k], device(zh=p)) for k, p in enumerate(zh_peers)
        ])

    def do_sz(r):
        arrive(("sx", r))
        total = xsum32[r, zh]
        for k in range(3):
            total = total + z_got[r, k].astype(F32)
        wide[r, x, zh] = (total * weights[r % 2, zh][:, 0:1]).astype(BF)
        mine = wide.at[r, x, zh]
        send(("sz", r), wide.at[r, x, pl.ds(0, 3)], [(mine, mine, device(zh=p)) for p in zh_peers])

    def do_gx(r):
        arrive(("sz", r))
        mine = wide.at[r, x]
        send(("gx", r), wide.at[r, pl.ds(0, 3)], [(mine, mine, device(x=p)) for p in x_peers])

    def do_turn(r):
        arrive(("gx", r))
        h, b = divmod(r, 2)
        wide_t[h, :, b * TOK : (b + 1) * TOK] = jnp.transpose(wide[r].reshape(TOK, QUARTER))

    def do_fz():
        mine = rows_up.at[:, :, zh, x]
        send(("fz",), rows_up.at[:, :, pl.ds(0, 3), x], [
            (mine, mine, device(zh=p)) for p in zh_peers
        ])

    def do_fx():
        arrive(("fz",))
        mine = rows_up.at[:, :, :, x]
        send(("fx",), rows_up.at[:, :, :, pl.ds(0, 3)], [(mine, mine, device(x=p)) for p in x_peers])

    def do_mm2(e):
        h, start, width = PARTS[e]
        g_own, ysum, y_got = of_part[e][0:3]
        if ("gin",) in flying:
            arrive(("gin",))
        rhs = g_in[...].reshape(2 * TOK, FF)[:, start : start + width]
        value = jnp.dot(wide_t[h], rhs, preferred_element_type=F32)
        g_own[...] = value.reshape(4, 4, 16, width)
        for k, p in enumerate(y_peers):
            ysum[k] = g_own[p].astype(BF)
        send(("mm2", e), y_got, [
            (ysum.at[k], y_got.at[k], device(y=p)) for k, p in enumerate(y_peers)
        ])

    def do_sy(e):
        g_own, _, y_got, zsum32, zsum, l_got = of_part[e][0:6]
        total = g_own[y]
        arrive(("mm2", e))
        for k in range(3):
            total = total + y_got[k].astype(F32)
        zsum32[...] = total
        zsum[...] = total.astype(BF)
        send(("sy", e), l_got, [
            (zsum.at[p], l_got.at[k], device(zl=p)) for k, p in enumerate(zl_peers)
        ])

    def do_adam(e):
        h, start, width = PARTS[e]
        zsum32, _, l_got, full = of_part[e][3:7]
        rows, cols = pl.ds(h * 16, 16), pl.ds(start, width)
        arrive(("sy", e))
        grad = zsum32[zl]
        for k in range(3):
            grad = grad + l_got[k].astype(F32)
        for cp in loads[2:]:
            cp.wait()
        del loads[2:]
        first = beta_first * m_in[rows, cols] + (1.0 - beta_first) * grad
        second = beta_second * v_in[rows, cols] + (1.0 - beta_second) * (grad * grad)
        way = first / bias_first / (jnp.sqrt(second / bias_second) + epsilon)
        full[core, y, zl] = way.astype(BF)
        mine = full.at[core, y, zl]
        send(("adam", e), full.at[core, y, pl.ds(0, 3)], [
            (mine, mine, device(zl=p)) for p in zl_peers
        ])
        m_new[rows, cols] = first
        v_new[rows, cols] = second

    def do_gy(e):
        full = of_part[e][6]
        arrive(("adam", e))
        mine = full.at[core, y]
        send(("gy", e), full.at[core, pl.ds(0, 3)], [(mine, mine, device(y=p)) for p in y_peers])

    def do_gc(e):
        full = of_part[e][6]
        arrive(("gy", e))
        mine = full.at[core]
        send(("gc", e), mine, [(mine, mine, device(core=other))])

    def do_up(e):
        h, start, width = PARTS[e]
        full = of_part[e][6]
        if ("fx",) in flying:
            arrive(("fx",))
        value = jnp.dot(
            rows_up[h, core].reshape(256, QUARTER), full[core].reshape(QUARTER, width),
            preferred_element_type=F32,
        )
        arrive(("gc", e))
        value = value + jnp.dot(
            rows_up[h, other].reshape(256, QUARTER), full[other].reshape(QUARTER, width),
            preferred_element_type=F32,
        )
        if h == 0:
            u_sum[:, pl.ds(start, width)] = value
        else:
            value = value + u_sum[:, pl.ds(start, width)]
            u_new[:, pl.ds(start, width)] = value.astype(BF)

    steps = {
        "hop": do_hop, "zl": do_zl, "cnt": do_cnt, "mm": do_mm, "sx": do_sx,
        "sz": do_sz, "gx": do_gx, "turn": do_turn, "fz": do_fz, "fx": do_fx, "mm2": do_mm2,
        "sy": do_sy, "adam": do_adam, "gy": do_gy, "gc": do_gc, "up": do_up,
    }
    for name, *which in ORDER:
        steps[name](*which)

    outs = [
        pltpu.make_async_copy(value, out, loc_sem.at[i])
        for i, (value, out) in enumerate(((m_new, m_out), (v_new, v_out), (u_new, u_out)))
    ]
    for cp in outs:
        cp.start()

    @pl.when(moves)
    def _():
        for h in range(2):
            for c in range(2):
                hop_wait(h, c, send_sem)

    @pl.when(jnp.logical_not(moves))
    def _():
        for h in range(2):
            hop_wait(h, other, send_sem)

    for whole, i in groups:
        pltpu.make_async_copy(whole, whole, send_sem.at[i]).wait()
    for cp in outs:
        cp.wait()


def hand_on(m_in, v_in, u_in, m_out, v_out, u_out, m_held, v_held, u_held, sem):
    ways = ((m_in, m_held, m_out), (v_in, v_held, v_out), (u_in, u_held, u_out))
    reads = [pltpu.make_async_copy(a, b, sem.at[i]) for i, (a, b, _) in enumerate(ways)]
    writes = [pltpu.make_async_copy(b, c, sem.at[3 + i]) for i, (_, b, c) in enumerate(ways)]
    for cp in reads:
        cp.start()
    for read, write in zip(reads, writes):
        read.wait()
        write.start()
    for cp in writes:
        cp.wait()


def local(layer_input, out_grad, projector, first_moment, second_moment, doc_ids):
    scratch = [
        pltpu.VMEM((2, TOK, FEAT), BF),
        pltpu.VMEM((2, TOK, FF), BF),
        pltpu.VMEM((MOM, FF), F32),
        pltpu.VMEM((MOM, FF), F32),
        pltpu.VMEM((ROWS, RANK), BF),
        pltpu.VMEM((2, 2, 4, 4, ROWS, QUARTER), BF),
        pltpu.VMEM((2, 2, 4, 4, ROWS, QUARTER), BF),
        pltpu.VMEM((4, 4, 4, SUB, QUARTER), F32),
        pltpu.VMEM((4, 4, 4, SUB, QUARTER), BF),
        pltpu.VMEM((4, 3, 4, SUB, QUARTER), BF),
        pltpu.VMEM((4, 4, SUB, QUARTER), F32),
        pltpu.VMEM((4, 4, SUB, QUARTER), BF),
        pltpu.VMEM((4, 3, SUB, QUARTER), BF),
        pltpu.VMEM((4, 4, 4, SUB, QUARTER), BF),
        pltpu.VMEM((2, QUARTER, 2 * TOK), BF),
        pltpu.VMEM((3, 8, 128), F32),
        pltpu.VMEM((7, 8, 128), F32),
        pltpu.VMEM((2, 1, TOK), jnp.int32),
        pltpu.VMEM((256, FF), F32),
        pltpu.SemaphoreType.DMA((5,)),
        pltpu.SemaphoreType.DMA((N_SEM,)),
        pltpu.SemaphoreType.DMA((N_SEM,)),
    ]
    for _, _, w in PARTS:
        scratch += [
            pltpu.VMEM((4, 4, 16, w), F32),
            pltpu.VMEM((3, 4, 16, w), BF),
            pltpu.VMEM((3, 4, 16, w), BF),
            pltpu.VMEM((4, 16, w), F32),
            pltpu.VMEM((4, 16, w), BF),
            pltpu.VMEM((3, 16, w), BF),
            pltpu.VMEM((2, 4, 4, 16, w), BF),
        ]
    scratch += [
        pltpu.VMEM((MOM, FF), F32),
        pltpu.VMEM((MOM, FF), F32),
        pltpu.VMEM((256, FF), BF),
        pltpu.VMEM((2, 4, SUB, 128), F32),
    ]
    any_space = pl.BlockSpec(memory_space=pl.ANY)
    results = (
        jax.ShapeDtypeStruct((MOM, FF), F32),
        jax.ShapeDtypeStruct((MOM, FF), F32),
        jax.ShapeDtypeStruct((256, FF), BF),
    )
    made = pl.pallas_call(
        kernel,
        out_shape=results,
        in_specs=[any_space] * 5 + [pl.BlockSpec(memory_space=pltpu.VMEM)],
        out_specs=(any_space,) * 3,
        scratch_shapes=scratch,
        compiler_params=pltpu.CompilerParams(
            collective_id=0, has_side_effects=True, vmem_limit_bytes=56 * 2**20
        ),
        cost_estimate=pl.CostEstimate(flops=2 * 10**9, bytes_accessed=4 * 10**6, transcendentals=0),
        name="galore",
    )(layer_input, out_grad, projector, first_moment, second_moment, doc_ids.reshape(1, TOK))
    return pl.pallas_call(
        hand_on,
        out_shape=results,
        in_specs=[any_space] * 3,
        out_specs=(any_space,) * 3,
        scratch_shapes=[
            pltpu.VMEM((MOM, FF), F32),
            pltpu.VMEM((MOM, FF), F32),
            pltpu.VMEM((256, FF), BF),
            pltpu.SemaphoreType.DMA((6,)),
        ],
        compiler_params=pltpu.CompilerParams(vmem_limit_bytes=56 * 2**20),
        name="hand_on",
    )(*made)


def solution(mesh):
    placed = (
        P("dp", "shard"),
        P("dp", "shard"),
        P(("dp", "shard"), None),
        P("dp", "shard"),
        P("dp", "shard"),
        P("dp"),
    )
    return jax.shard_map(
        local,
        mesh=mesh,
        in_specs=placed,
        out_specs=(P("dp", "shard"), P("dp", "shard"), P("dp", "shard")),
        check_vma=False,
    )
```

```python
import jax
import jax.numpy as jnp
from jax import lax
from jax.experimental import pallas as pl
from jax.experimental.pallas import tpu as pltpu
from jax.sharding import PartitionSpec as P

MESH = pl.DeviceIdType.MESH
BF = jnp.bfloat16
F32 = jnp.float32

beta_first = 0.9
beta_second = 0.95
bias_first = 1.0 - beta_first**2
bias_second = 1.0 - beta_second**2
epsilon = 1e-08

TOK, FEAT, RANK, FF, ROWS, MOM = 512, 512, 1024, 896, 16, 32
HALF = RANK // 2
QUARTER = RANK // 4
SUB = TOK // 16
PARTS = ((0, 0, 896), (1, 0, 384), (1, 384, 512))
N_PARTS = len(PARTS)
ORDER = (
    ("cnt", 0), ("hop", 0), ("cnt", 1), ("hop", 1), ("cnt", 2), ("zl", 0), ("zl", 1), ("mm", 1), ("mm", 0),
    ("mm", 3), ("mm", 2), ("sx", 1), ("sx", 0), ("sx", 3), ("sz", 1), ("sx", 2), ("sz", 0), ("sz", 3),
    ("gx", 1), ("sz", 2), ("gx", 0), ("gx", 3), ("turn", 1), ("gx", 2), ("fz",), ("turn", 0), ("mm2", 0),
    ("turn", 3), ("turn", 2), ("mm2", 2), ("mm2", 1), ("fx",), ("sy", 0), ("sy", 2), ("adam", 0), ("sy", 1),
    ("adam", 2), ("gy", 0), ("adam", 1), ("gy", 2), ("gy", 1), ("gc", 0), ("up", 0), ("gc", 2), ("gc", 1),
    ("up", 2), ("up", 1),
)
N_SEM = 34 + 5 * N_PARTS
N_FIXED = 22
N_EACH = 7


def kernel(x_hbm, g_hbm, p_hbm, m_hbm, v_hbm, ids_ref, m_out, v_out, u_out, *scratch):
    (
        x_in, g_in, m_in, v_in, p_in, rows_in, rows_up,
        part32, part, x_got, xsum32, xsum, z_got, wide, wide_t,
        count, count_got, ids_all, u_sum,
        loc_sem, send_sem, recv_sem,
    ) = scratch[:N_FIXED]
    of_part = [scratch[N_FIXED + N_EACH * e : N_FIXED + N_EACH * (e + 1)] for e in range(N_PARTS)]
    m_new, v_new, u_new, weights = scratch[N_FIXED + N_EACH * N_PARTS :]

    d, s = lax.axis_index("dp"), lax.axis_index("shard")
    core = lax.rem(d, 2)
    zl = lax.rem(lax.div(d, 2), 4)
    y = lax.div(d, 8)
    x = lax.rem(s, 4)
    zh = lax.div(s, 4)

    def device(y=y, zl=zl, core=core, zh=zh, x=x):
        return ((y * 4 + zl) * 2 + core, zh * 4 + x)

    def up(value, k):
        return lax.rem(value + k, 4)

    other = 1 - core
    x_peers = [up(x, k) for k in (2, 1 + 2 * core, 3 - 2 * core)]
    y_peers = [up(y, k) for k in (2, 1 + 2 * core, 3 - 2 * core)]
    zl_peers = [up(zl, k) for k in (2, 1 + 2 * core, 3 - 2 * core)]
    zh_peers = [up(zh, k) for k in (2, 1 + 2 * core, 3 - 2 * core)]

    used = [0]
    flying = {}
    groups = []

    def send(name, whole, copies):
        i = used[0]
        used[0] += 1
        for src, dst, to in copies:
            pltpu.make_async_remote_copy(
                src_ref=src, dst_ref=dst, send_sem=send_sem.at[i], recv_sem=recv_sem.at[i],
                device_id=to, device_id_type=MESH,
            ).start()
        flying[name] = (whole, i)
        groups.append((whole, i))

    def arrive(name):
        whole, i = flying.pop(name)
        pltpu.make_async_copy(whole, whole, recv_sem.at[i]).wait()

    own_rows = pltpu.make_async_copy(p_hbm, p_in, loc_sem.at[0])
    loads = [
        pltpu.make_async_copy(x_hbm, x_in.at[core], loc_sem.at[1]),
        pltpu.make_async_copy(g_hbm, g_in.at[core], loc_sem.at[2]),
        pltpu.make_async_copy(m_hbm, m_in, loc_sem.at[3]),
        pltpu.make_async_copy(v_hbm, v_in, loc_sem.at[4]),
    ]
    own_rows.start()
    for cp in loads:
        cp.start()

    to_hop = [device(y=up(zh, y), zl=x, zh=y, x=zl, core=c) for c in range(2)]
    seat = up(y, 4 - zh)
    from_hop = [device(y=zh, zl=x, zh=seat, x=zl, core=c) for c in range(2)]
    moves = jnp.logical_or(x != zl, jnp.logical_or(y != 0, zh != 0))
    barrier = pltpu.get_barrier_semaphore()
    greet = [device(core=other)]
    greet += [device(x=p) for p in x_peers] + [device(y=p) for p in y_peers]
    greet += [device(zl=p) for p in zl_peers] + [device(zh=p) for p in zh_peers]
    for to in greet:
        pl.semaphore_signal(barrier, inc=1, device_id=to, device_id_type=MESH)

    @pl.when(moves)
    def _():
        for to in from_hop:
            pl.semaphore_signal(barrier, inc=1, device_id=to, device_id_type=MESH)

    own_rows.wait()
    held = p_in[...].astype(F32)
    turned = [held] + [jnp.concatenate([held[:, k:], held[:, :k]], axis=1) for k in (32, 16, 48)]
    turned = jnp.concatenate(turned, axis=0).astype(BF)
    at = lax.broadcasted_iota(jnp.int32, (RANK, QUARTER), 0)
    col = lax.broadcasted_iota(jnp.int32, (1, QUARTER), 1)
    pick = (at == (col >> 4) * 64 + (col & 15)).astype(F32).astype(BF)
    moved = jnp.dot(turned, pick, preferred_element_type=F32).astype(BF)
    for r in range(4):
        h, c = divmod(r, 2)
        rows_up[h, c, zh, x] = moved[r * ROWS : (r + 1) * ROWS]

    ids = jnp.transpose(jnp.broadcast_to(ids_ref[...], (128, TOK)))
    match = (ids == lax.broadcasted_iota(jnp.int32, (TOK, 128), 1)).astype(F32)
    count[0] = jnp.broadcast_to(jnp.sum(match, axis=0, keepdims=True), (8, 128))

    pl.semaphore_wait(barrier, len(greet) + 2 * moves.astype(jnp.int32))

    def hop(h, c):
        i = N_SEM - 1 - (2 * h + c)
        return pltpu.make_async_remote_copy(
            src_ref=rows_up.at[h, c, zh, x], dst_ref=rows_in.at[h, core, zh, x],
            send_sem=send_sem.at[i], recv_sem=recv_sem.at[N_SEM - 1 - (2 * h + core)],
            device_id=to_hop[c], device_id_type=MESH,
        )

    def stay(h):
        return pltpu.make_async_remote_copy(
            src_ref=rows_up.at[h, other, zh, x], dst_ref=rows_in.at[h, core, zh, x],
            send_sem=send_sem.at[N_SEM - 1 - (2 * h + other)],
            recv_sem=recv_sem.at[N_SEM - 1 - (2 * h + core)],
            device_id=device(core=other), device_id_type=MESH,
        )

    def hop_wait(h, c, sems):
        whole = rows_up.at[h, c, zh, x]
        pltpu.make_async_copy(whole, whole, sems.at[N_SEM - 1 - (2 * h + c)]).wait()

    @pl.when(moves)
    def _():
        for h in range(2):
            for c in range(2):
                hop(h, c).start()

    @pl.when(jnp.logical_not(moves))
    def _():
        for h in range(2):
            stay(h).start()
            rows_in[h, core, zh, x] = rows_up[h, core, zh, x]

    for cp in loads[:2]:
        cp.wait()
    to = device(core=other)
    ids_all[core] = ids_ref[...]
    send(("CNT", 0), count_got.at[0], [(count.at[0], count_got.at[0], to)])
    send(("ids",), ids_all.at[0], [(ids_all.at[core], ids_all.at[core], to)])
    send(("xin",), x_in.at[0], [(x_in.at[core], x_in.at[core], to)])
    send(("gin",), g_in.at[0], [(g_in.at[core], g_in.at[core], to)])

    def do_cnt(i):
        if i == 0:
            arrive(("CNT", 0))
            count[1] = count[0] + count_got[0]
            send(("cnt", 0), count_got.at[pl.ds(1, 3)], [
                (count.at[1], count_got.at[1 + k], device(zl=p)) for k, p in enumerate(zl_peers)
            ])
        elif i == 1:
            arrive(("cnt", 0))
            count[2] = count[1] + count_got[1] + count_got[2] + count_got[3]
            send(("cnt", 1), count_got.at[pl.ds(4, 3)], [
                (count.at[2], count_got.at[4 + k], device(y=p)) for k, p in enumerate(y_peers)
            ])
        else:
            arrive(("cnt", 1))
            lengths = count[2] + count_got[4] + count_got[5] + count_got[6]
            inverse = 1.0 / lengths[0:1]
            arrive(("ids",))
            for b in range(2):
                mine = ids_all[b, :, pl.ds(pl.multiple_of(x * 128, 128), 128)]
                mine = jnp.transpose(jnp.broadcast_to(mine, (128, 128)))
                here = mine == lax.broadcasted_iota(jnp.int32, (128, 128), 1)
                weight = jnp.sum(jnp.where(here, inverse, 0.0), axis=1, keepdims=True)
                weights[b] = jnp.broadcast_to(weight, (128, 128)).reshape(4, SUB, 128)

    def do_hop(h):
        @pl.when(moves)
        def _():
            for c in range(2):
                hop_wait(h, c, recv_sem)

        @pl.when(jnp.logical_not(moves))
        def _():
            hop_wait(h, other, recv_sem)

        mine = rows_in.at[h, :, seat, zl]
        send(("hop", h), rows_in.at[h, :, 0, pl.ds(0, 3)], [
            (mine, mine, device(zl=p)) for p in zl_peers
        ])

    def do_zl(h):
        arrive(("hop", h))
        mine = rows_in.at[h, :, seat]
        send(("zl", h), rows_in.at[h, :, pl.ds(0, 3)], [
            (mine, mine, device(y=p)) for p in y_peers
        ])

    def do_mm(r):
        h, b = divmod(r, 2)
        for name in (("zl", h), ("xin",)):
            if name in flying:
                arrive(name)
        rhs = rows_in[h].reshape(FEAT, QUARTER)
        value = jnp.dot(x_in[b], rhs, preferred_element_type=F32).reshape(4, 4, SUB, QUARTER)
        part32[r] = value
        part[r] = value.astype(BF)
        send(("mm", r), x_got.at[r], [
            (part.at[r, p], x_got.at[r, k], device(x=p)) for k, p in enumerate(x_peers)
        ])

    def do_sx(r):
        arrive(("mm", r))
        total = part32[r, x]
        for k in range(3):
            total = total + x_got[r, k].astype(F32)
        xsum32[r] = total
        xsum[r] = total.astype(BF)
        send(("sx", r), z_got.at[r], [
            (xsum.at[r, p], z_got.at[r, k], device(zh=p)) for k, p in enumerate(zh_peers)
        ])

    def do_sz(r):
        arrive(("sx", r))
        total = xsum32[r, zh]
        for k in range(3):
            total = total + z_got[r, k].astype(F32)
        wide[r, x, zh] = (total * weights[r % 2, zh][:, 0:1]).astype(BF)
        mine = wide.at[r, x, zh]
        send(("sz", r), wide.at[r, x, pl.ds(0, 3)], [(mine, mine, device(zh=p)) for p in zh_peers])

    def do_gx(r):
        arrive(("sz", r))
        mine = wide.at[r, x]
        send(("gx", r), wide.at[r, pl.ds(0, 3)], [(mine, mine, device(x=p)) for p in x_peers])

    def do_turn(r):
        arrive(("gx", r))
        h, b = divmod(r, 2)
        wide_t[h, :, b * TOK : (b + 1) * TOK] = jnp.transpose(wide[r].reshape(TOK, QUARTER))

    def do_fz():
        mine = rows_up.at[:, :, zh, x]
        send(("fz",), rows_up.at[:, :, pl.ds(0, 3), x], [
            (mine, mine, device(zh=p)) for p in zh_peers
        ])

    def do_fx():
        arrive(("fz",))
        mine = rows_up.at[:, :, :, x]
        send(("fx",), rows_up.at[:, :, :, pl.ds(0, 3)], [(mine, mine, device(x=p)) for p in x_peers])

    def do_mm2(e):
        h, start, width = PARTS[e]
        g_own, ysum, y_got = of_part[e][0:3]
        if ("gin",) in flying:
            arrive(("gin",))
        rhs = g_in[...].reshape(2 * TOK, FF)[:, start : start + width]
        value = jnp.dot(wide_t[h], rhs, preferred_element_type=F32)
        g_own[...] = value.reshape(4, 4, 16, width)
        for k, p in enumerate(y_peers):
            ysum[k] = g_own[p].astype(BF)
        send(("mm2", e), y_got, [
            (ysum.at[k], y_got.at[k], device(y=p)) for k, p in enumerate(y_peers)
        ])

    def do_sy(e):
        g_own, _, y_got, zsum32, zsum, l_got = of_part[e][0:6]
        total = g_own[y]
        arrive(("mm2", e))
        for k in range(3):
            total = total + y_got[k].astype(F32)
        zsum32[...] = total
        zsum[...] = total.astype(BF)
        send(("sy", e), l_got, [
            (zsum.at[p], l_got.at[k], device(zl=p)) for k, p in enumerate(zl_peers)
        ])

    def do_adam(e):
        h, start, width = PARTS[e]
        zsum32, _, l_got, full = of_part[e][3:7]
        rows, cols = pl.ds(h * 16, 16), pl.ds(start, width)
        arrive(("sy", e))
        grad = zsum32[zl]
        for k in range(3):
            grad = grad + l_got[k].astype(F32)
        for cp in loads[2:]:
            cp.wait()
        del loads[2:]
        first = beta_first * m_in[rows, cols] + (1.0 - beta_first) * grad
        second = beta_second * v_in[rows, cols] + (1.0 - beta_second) * (grad * grad)
        way = first / bias_first / (jnp.sqrt(second / bias_second) + epsilon)
        full[core, y, zl] = way.astype(BF)
        mine = full.at[core, y, zl]
        send(("adam", e), full.at[core, y, pl.ds(0, 3)], [
            (mine, mine, device(zl=p)) for p in zl_peers
        ])
        m_new[rows, cols] = first
        v_new[rows, cols] = second

    def do_gy(e):
        full = of_part[e][6]
        arrive(("adam", e))
        mine = full.at[core, y]
        send(("gy", e), full.at[core, pl.ds(0, 3)], [(mine, mine, device(y=p)) for p in y_peers])

    def do_gc(e):
        full = of_part[e][6]
        arrive(("gy", e))
        mine = full.at[core]
        send(("gc", e), mine, [(mine, mine, device(core=other))])

    def do_up(e):
        h, start, width = PARTS[e]
        full = of_part[e][6]
        if ("fx",) in flying:
            arrive(("fx",))
        value = jnp.dot(
            rows_up[h, core].reshape(256, QUARTER), full[core].reshape(QUARTER, width),
            preferred_element_type=F32,
        )
        arrive(("gc", e))
        value = value + jnp.dot(
            rows_up[h, other].reshape(256, QUARTER), full[other].reshape(QUARTER, width),
            preferred_element_type=F32,
        )
        if h == 0:
            u_sum[:, pl.ds(start, width)] = value
        else:
            value = value + u_sum[:, pl.ds(start, width)]
            u_new[:, pl.ds(start, width)] = value.astype(BF)

    steps = {
        "hop": do_hop, "zl": do_zl, "cnt": do_cnt, "mm": do_mm, "sx": do_sx,
        "sz": do_sz, "gx": do_gx, "turn": do_turn, "fz": do_fz, "fx": do_fx, "mm2": do_mm2,
        "sy": do_sy, "adam": do_adam, "gy": do_gy, "gc": do_gc, "up": do_up,
    }
    for name, *which in ORDER:
        steps[name](*which)

    outs = [
        pltpu.make_async_copy(value, out, loc_sem.at[i])
        for i, (value, out) in enumerate(((m_new, m_out), (v_new, v_out), (u_new, u_out)))
    ]
    for cp in outs:
        cp.start()

    @pl.when(moves)
    def _():
        for h in range(2):
            for c in range(2):
                hop_wait(h, c, send_sem)

    @pl.when(jnp.logical_not(moves))
    def _():
        for h in range(2):
            hop_wait(h, other, send_sem)

    for whole, i in groups:
        pltpu.make_async_copy(whole, whole, send_sem.at[i]).wait()
    for cp in outs:
        cp.wait()


def hand_on(m_in, v_in, u_in, m_out, v_out, u_out, m_held, v_held, u_held, sem):
    ways = ((m_in, m_held, m_out), (v_in, v_held, v_out), (u_in, u_held, u_out))
    reads = [pltpu.make_async_copy(a, b, sem.at[i]) for i, (a, b, _) in enumerate(ways)]
    writes = [pltpu.make_async_copy(b, c, sem.at[3 + i]) for i, (_, b, c) in enumerate(ways)]
    for cp in reads:
        cp.start()
    for read, write in zip(reads, writes):
        read.wait()
        write.start()
    for cp in writes:
        cp.wait()


def local(layer_input, out_grad, projector, first_moment, second_moment, doc_ids):
    scratch = [
        pltpu.VMEM((2, TOK, FEAT), BF),
        pltpu.VMEM((2, TOK, FF), BF),
        pltpu.VMEM((MOM, FF), F32),
        pltpu.VMEM((MOM, FF), F32),
        pltpu.VMEM((ROWS, RANK), BF),
        pltpu.VMEM((2, 2, 4, 4, ROWS, QUARTER), BF),
        pltpu.VMEM((2, 2, 4, 4, ROWS, QUARTER), BF),
        pltpu.VMEM((4, 4, 4, SUB, QUARTER), F32),
        pltpu.VMEM((4, 4, 4, SUB, QUARTER), BF),
        pltpu.VMEM((4, 3, 4, SUB, QUARTER), BF),
        pltpu.VMEM((4, 4, SUB, QUARTER), F32),
        pltpu.VMEM((4, 4, SUB, QUARTER), BF),
        pltpu.VMEM((4, 3, SUB, QUARTER), BF),
        pltpu.VMEM((4, 4, 4, SUB, QUARTER), BF),
        pltpu.VMEM((2, QUARTER, 2 * TOK), BF),
        pltpu.VMEM((3, 8, 128), F32),
        pltpu.VMEM((7, 8, 128), F32),
        pltpu.VMEM((2, 1, TOK), jnp.int32),
        pltpu.VMEM((256, FF), F32),
        pltpu.SemaphoreType.DMA((5,)),
        pltpu.SemaphoreType.DMA((N_SEM,)),
        pltpu.SemaphoreType.DMA((N_SEM,)),
    ]
    for _, _, w in PARTS:
        scratch += [
            pltpu.VMEM((4, 4, 16, w), F32),
            pltpu.VMEM((3, 4, 16, w), BF),
            pltpu.VMEM((3, 4, 16, w), BF),
            pltpu.VMEM((4, 16, w), F32),
            pltpu.VMEM((4, 16, w), BF),
            pltpu.VMEM((3, 16, w), BF),
            pltpu.VMEM((2, 4, 4, 16, w), BF),
        ]
    scratch += [
        pltpu.VMEM((MOM, FF), F32),
        pltpu.VMEM((MOM, FF), F32),
        pltpu.VMEM((256, FF), BF),
        pltpu.VMEM((2, 4, SUB, 128), F32),
    ]
    any_space = pl.BlockSpec(memory_space=pl.ANY)
    results = (
        jax.ShapeDtypeStruct((MOM, FF), F32),
        jax.ShapeDtypeStruct((MOM, FF), F32),
        jax.ShapeDtypeStruct((256, FF), BF),
    )
    made = pl.pallas_call(
        kernel,
        out_shape=results,
        in_specs=[any_space] * 5 + [pl.BlockSpec(memory_space=pltpu.VMEM)],
        out_specs=(any_space,) * 3,
        scratch_shapes=scratch,
        compiler_params=pltpu.CompilerParams(
            collective_id=0, has_side_effects=True, vmem_limit_bytes=56 * 2**20
        ),
        cost_estimate=pl.CostEstimate(flops=2 * 10**9, bytes_accessed=4 * 10**6, transcendentals=0),
        name="galore",
    )(layer_input, out_grad, projector, first_moment, second_moment, doc_ids.reshape(1, TOK))
    return pl.pallas_call(
        hand_on,
        out_shape=results,
        in_specs=[any_space] * 3,
        out_specs=(any_space,) * 3,
        scratch_shapes=[
            pltpu.VMEM((MOM, FF), F32),
            pltpu.VMEM((MOM, FF), F32),
            pltpu.VMEM((256, FF), BF),
            pltpu.SemaphoreType.DMA((6,)),
        ],
        compiler_params=pltpu.CompilerParams(vmem_limit_bytes=56 * 2**20),
        name="hand_on",
    )(*made)


def solution(mesh):
    placed = (
        P("dp", "shard"),
        P("dp", "shard"),
        P(("dp", "shard"), None),
        P("dp", "shard"),
        P("dp", "shard"),
        P("dp"),
    )
    return jax.shard_map(
        local,
        mesh=mesh,
        in_specs=placed,
        out_specs=(P("dp", "shard"), P("dp", "shard"), P("dp", "shard")),
        check_vma=False,
    )
```

```python
import jax
import jax.numpy as jnp
from jax import lax
from jax.experimental import pallas as pl
from jax.experimental.pallas import tpu as pltpu
from jax.sharding import PartitionSpec as P

MESH = pl.DeviceIdType.MESH
BF = jnp.bfloat16
F32 = jnp.float32

beta_first = 0.9
beta_second = 0.95
bias_first = 1.0 - beta_first**2
bias_second = 1.0 - beta_second**2
epsilon = 1e-08

TOK, FEAT, RANK, FF, ROWS, MOM = 512, 512, 1024, 896, 16, 32
HALF = RANK // 2
QUARTER = RANK // 4
SUB = TOK // 16
PARTS = ((0, 0, 896), (1, 0, 384), (1, 384, 512))
N_PARTS = len(PARTS)
ORDER = (
    ("cnt", 0), ("hop", 0), ("cnt", 1), ("hop", 1), ("cnt", 2), ("zl", 0), ("zl", 1), ("mm", 1), ("mm", 0),
    ("mm", 3), ("mm", 2), ("sx", 1), ("sx", 0), ("sx", 3), ("sz", 1), ("sx", 2), ("sz", 0), ("sz", 3),
    ("gx", 1), ("sz", 2), ("gx", 0), ("gx", 3), ("turn", 1), ("gx", 2), ("fz",), ("turn", 0), ("mm2", 0),
    ("turn", 3), ("turn", 2), ("mm2", 2), ("mm2", 1), ("fx",), ("sy", 0), ("sy", 2), ("adam", 0), ("sy", 1),
    ("adam", 2), ("gy", 0), ("adam", 1), ("gy", 2), ("gy", 1), ("gc", 0), ("up", 0), ("gc", 2), ("gc", 1),
    ("up", 2), ("up", 1),
)
N_SEM = 34 + 5 * N_PARTS
N_FIXED = 22
N_EACH = 7


def kernel(x_hbm, g_hbm, p_hbm, m_hbm, v_hbm, ids_ref, m_out, v_out, u_out, *scratch):
    (
        x_in, g_in, m_in, v_in, p_in, rows_in, rows_up,
        part32, part, x_got, xsum32, xsum, z_got, wide, wide_t,
        count, count_got, ids_all, u_sum,
        loc_sem, send_sem, recv_sem,
    ) = scratch[:N_FIXED]
    of_part = [scratch[N_FIXED + N_EACH * e : N_FIXED + N_EACH * (e + 1)] for e in range(N_PARTS)]
    m_new, v_new, u_new, weights = scratch[N_FIXED + N_EACH * N_PARTS :]

    d, s = lax.axis_index("dp"), lax.axis_index("shard")
    core = lax.rem(d, 2)
    zl = lax.rem(lax.div(d, 2), 4)
    y = lax.div(d, 8)
    x = lax.rem(s, 4)
    zh = lax.div(s, 4)

    def device(y=y, zl=zl, core=core, zh=zh, x=x):
        return ((y * 4 + zl) * 2 + core, zh * 4 + x)

    def up(value, k):
        return lax.rem(value + k, 4)

    other = 1 - core
    x_peers = [up(x, k) for k in (2, 1 + 2 * core, 3 - 2 * core)]
    y_peers = [up(y, k) for k in (2, 1 + 2 * core, 3 - 2 * core)]
    zl_peers = [up(zl, k) for k in (2, 1 + 2 * core, 3 - 2 * core)]
    zh_peers = [up(zh, k) for k in (2, 1 + 2 * core, 3 - 2 * core)]

    used = [0]
    flying = {}
    groups = []

    def send(name, whole, copies):
        i = used[0]
        used[0] += 1
        for src, dst, to in copies:
            pltpu.make_async_remote_copy(
                src_ref=src, dst_ref=dst, send_sem=send_sem.at[i], recv_sem=recv_sem.at[i],
                device_id=to, device_id_type=MESH,
            ).start()
        flying[name] = (whole, i)
        groups.append((whole, i))

    def arrive(name):
        whole, i = flying.pop(name)
        pltpu.make_async_copy(whole, whole, recv_sem.at[i]).wait()

    own_rows = pltpu.make_async_copy(p_hbm, p_in, loc_sem.at[0])
    loads = [
        pltpu.make_async_copy(x_hbm, x_in.at[core], loc_sem.at[1]),
        pltpu.make_async_copy(g_hbm, g_in.at[core], loc_sem.at[2]),
        pltpu.make_async_copy(m_hbm, m_in, loc_sem.at[3]),
        pltpu.make_async_copy(v_hbm, v_in, loc_sem.at[4]),
    ]
    own_rows.start()
    for cp in loads:
        cp.start()

    to_hop = [device(y=up(zh, y), zl=x, zh=y, x=zl, core=c) for c in range(2)]
    seat = up(y, 4 - zh)
    from_hop = [device(y=zh, zl=x, zh=seat, x=zl, core=c) for c in range(2)]
    moves = jnp.logical_or(x != zl, jnp.logical_or(y != 0, zh != 0))
    barrier = pltpu.get_barrier_semaphore()
    greet = [device(core=other)]
    greet += [device(x=p) for p in x_peers] + [device(y=p) for p in y_peers]
    greet += [device(zl=p) for p in zl_peers] + [device(zh=p) for p in zh_peers]
    for to in greet:
        pl.semaphore_signal(barrier, inc=1, device_id=to, device_id_type=MESH)

    @pl.when(moves)
    def _():
        for to in from_hop:
            pl.semaphore_signal(barrier, inc=1, device_id=to, device_id_type=MESH)

    own_rows.wait()
    held = p_in[...].astype(F32)
    turned = [held] + [jnp.concatenate([held[:, k:], held[:, :k]], axis=1) for k in (32, 16, 48)]
    turned = jnp.concatenate(turned, axis=0).astype(BF)
    at = lax.broadcasted_iota(jnp.int32, (RANK, QUARTER), 0)
    col = lax.broadcasted_iota(jnp.int32, (1, QUARTER), 1)
    pick = (at == (col >> 4) * 64 + (col & 15)).astype(F32).astype(BF)
    moved = jnp.dot(turned, pick, preferred_element_type=F32).astype(BF)
    for r in range(4):
        h, c = divmod(r, 2)
        rows_up[h, c, zh, x] = moved[r * ROWS : (r + 1) * ROWS]

    ids = jnp.transpose(jnp.broadcast_to(ids_ref[...], (128, TOK)))
    match = (ids == lax.broadcasted_iota(jnp.int32, (TOK, 128), 1)).astype(F32)
    count[0] = jnp.broadcast_to(jnp.sum(match, axis=0, keepdims=True), (8, 128))

    pl.semaphore_wait(barrier, len(greet) + 2 * moves.astype(jnp.int32))

    def hop(h, c):
        i = N_SEM - 1 - (2 * h + c)
        return pltpu.make_async_remote_copy(
            src_ref=rows_up.at[h, c, zh, x], dst_ref=rows_in.at[h, core, zh, x],
            send_sem=send_sem.at[i], recv_sem=recv_sem.at[N_SEM - 1 - (2 * h + core)],
            device_id=to_hop[c], device_id_type=MESH,
        )

    def stay(h):
        return pltpu.make_async_remote_copy(
            src_ref=rows_up.at[h, other, zh, x], dst_ref=rows_in.at[h, core, zh, x],
            send_sem=send_sem.at[N_SEM - 1 - (2 * h + other)],
            recv_sem=recv_sem.at[N_SEM - 1 - (2 * h + core)],
            device_id=device(core=other), device_id_type=MESH,
        )

    def hop_wait(h, c, sems):
        whole = rows_up.at[h, c, zh, x]
        pltpu.make_async_copy(whole, whole, sems.at[N_SEM - 1 - (2 * h + c)]).wait()

    @pl.when(moves)
    def _():
        for h in range(2):
            for c in range(2):
                hop(h, c).start()

    @pl.when(jnp.logical_not(moves))
    def _():
        for h in range(2):
            stay(h).start()
            rows_in[h, core, zh, x] = rows_up[h, core, zh, x]

    for cp in loads[:2]:
        cp.wait()
    to = device(core=other)
    ids_all[core] = ids_ref[...]
    send(("CNT", 0), count_got.at[0], [(count.at[0], count_got.at[0], to)])
    send(("ids",), ids_all.at[0], [(ids_all.at[core], ids_all.at[core], to)])
    send(("xin",), x_in.at[0], [(x_in.at[core], x_in.at[core], to)])
    send(("gin",), g_in.at[0], [(g_in.at[core], g_in.at[core], to)])

    def do_cnt(i):
        if i == 0:
            arrive(("CNT", 0))
            count[1] = count[0] + count_got[0]
            send(("cnt", 0), count_got.at[pl.ds(1, 3)], [
                (count.at[1], count_got.at[1 + k], device(zl=p)) for k, p in enumerate(zl_peers)
            ])
        elif i == 1:
            arrive(("cnt", 0))
            count[2] = count[1] + count_got[1] + count_got[2] + count_got[3]
            send(("cnt", 1), count_got.at[pl.ds(4, 3)], [
                (count.at[2], count_got.at[4 + k], device(y=p)) for k, p in enumerate(y_peers)
            ])
        else:
            arrive(("cnt", 1))
            lengths = count[2] + count_got[4] + count_got[5] + count_got[6]
            inverse = 1.0 / lengths[0:1]
            arrive(("ids",))
            for b in range(2):
                mine = ids_all[b, :, pl.ds(pl.multiple_of(x * 128, 128), 128)]
                mine = jnp.transpose(jnp.broadcast_to(mine, (128, 128)))
                here = mine == lax.broadcasted_iota(jnp.int32, (128, 128), 1)
                weight = jnp.sum(jnp.where(here, inverse, 0.0), axis=1, keepdims=True)
                weights[b] = jnp.broadcast_to(weight, (128, 128)).reshape(4, SUB, 128)

    def do_hop(h):
        @pl.when(moves)
        def _():
            for c in range(2):
                hop_wait(h, c, recv_sem)

        @pl.when(jnp.logical_not(moves))
        def _():
            hop_wait(h, other, recv_sem)

        mine = rows_in.at[h, :, seat, zl]
        send(("hop", h), rows_in.at[h, :, 0, pl.ds(0, 3)], [
            (mine, mine, device(zl=p)) for p in zl_peers
        ])

    def do_zl(h):
        arrive(("hop", h))
        mine = rows_in.at[h, :, seat]
        send(("zl", h), rows_in.at[h, :, pl.ds(0, 3)], [
            (mine, mine, device(y=p)) for p in y_peers
        ])

    def do_mm(r):
        h, b = divmod(r, 2)
        for name in (("zl", h), ("xin",)):
            if name in flying:
                arrive(name)
        rhs = rows_in[h].reshape(FEAT, QUARTER)
        value = jnp.dot(x_in[b], rhs, preferred_element_type=F32).reshape(4, 4, SUB, QUARTER)
        part32[r] = value
        part[r] = value.astype(BF)
        send(("mm", r), x_got.at[r], [
            (part.at[r, p], x_got.at[r, k], device(x=p)) for k, p in enumerate(x_peers)
        ])

    def do_sx(r):
        arrive(("mm", r))
        total = part32[r, x]
        for k in range(3):
            total = total + x_got[r, k].astype(F32)
        xsum32[r] = total
        xsum[r] = total.astype(BF)
        send(("sx", r), z_got.at[r], [
            (xsum.at[r, p], z_got.at[r, k], device(zh=p)) for k, p in enumerate(zh_peers)
        ])

    def do_sz(r):
        arrive(("sx", r))
        total = xsum32[r, zh]
        for k in range(3):
            total = total + z_got[r, k].astype(F32)
        wide[r, x, zh] = (total * weights[r % 2, zh][:, 0:1]).astype(BF)
        mine = wide.at[r, x, zh]
        send(("sz", r), wide.at[r, x, pl.ds(0, 3)], [(mine, mine, device(zh=p)) for p in zh_peers])

    def do_gx(r):
        arrive(("sz", r))
        mine = wide.at[r, x]
        send(("gx", r), wide.at[r, pl.ds(0, 3)], [(mine, mine, device(x=p)) for p in x_peers])

    def do_turn(r):
        arrive(("gx", r))
        h, b = divmod(r, 2)
        wide_t[h, :, b * TOK : (b + 1) * TOK] = jnp.transpose(wide[r].reshape(TOK, QUARTER))

    def do_fz():
        mine = rows_up.at[:, :, zh, x]
        send(("fz",), rows_up.at[:, :, pl.ds(0, 3), x], [
            (mine, mine, device(zh=p)) for p in zh_peers
        ])

    def do_fx():
        arrive(("fz",))
        mine = rows_up.at[:, :, :, x]
        send(("fx",), rows_up.at[:, :, :, pl.ds(0, 3)], [(mine, mine, device(x=p)) for p in x_peers])

    def do_mm2(e):
        h, start, width = PARTS[e]
        g_own, ysum, y_got = of_part[e][0:3]
        if ("gin",) in flying:
            arrive(("gin",))
        rhs = g_in[...].reshape(2 * TOK, FF)[:, start : start + width]
        value = jnp.dot(wide_t[h], rhs, preferred_element_type=F32)
        g_own[...] = value.reshape(4, 4, 16, width)
        for k, p in enumerate(y_peers):
            ysum[k] = g_own[p].astype(BF)
        send(("mm2", e), y_got, [
            (ysum.at[k], y_got.at[k], device(y=p)) for k, p in enumerate(y_peers)
        ])

    def do_sy(e):
        g_own, _, y_got, zsum32, zsum, l_got = of_part[e][0:6]
        total = g_own[y]
        arrive(("mm2", e))
        for k in range(3):
            total = total + y_got[k].astype(F32)
        zsum32[...] = total
        zsum[...] = total.astype(BF)
        send(("sy", e), l_got, [
            (zsum.at[p], l_got.at[k], device(zl=p)) for k, p in enumerate(zl_peers)
        ])

    stepped = []
    outs = [
        pltpu.make_async_copy(value, out, loc_sem.at[i])
        for i, (value, out) in enumerate(((m_new, m_out), (v_new, v_out)))
    ]

    def do_adam(e):
        h, start, width = PARTS[e]
        zsum32, _, l_got, full = of_part[e][3:7]
        rows, cols = pl.ds(h * 16, 16), pl.ds(start, width)
        arrive(("sy", e))
        grad = zsum32[zl]
        for k in range(3):
            grad = grad + l_got[k].astype(F32)
        for cp in loads[2:]:
            cp.wait()
        del loads[2:]
        first = beta_first * m_in[rows, cols] + (1.0 - beta_first) * grad
        second = beta_second * v_in[rows, cols] + (1.0 - beta_second) * (grad * grad)
        way = first / bias_first / (jnp.sqrt(second / bias_second) + epsilon)
        full[core, y, zl] = way.astype(BF)
        mine = full.at[core, y, zl]
        send(("adam", e), full.at[core, y, pl.ds(0, 3)], [
            (mine, mine, device(zl=p)) for p in zl_peers
        ])
        m_new[rows, cols] = first
        v_new[rows, cols] = second
        stepped.append(e)
        if len(stepped) == N_PARTS:
            for cp in outs[:2]:
                cp.start()

    def do_gy(e):
        full = of_part[e][6]
        arrive(("adam", e))
        mine = full.at[core, y]
        send(("gy", e), full.at[core, pl.ds(0, 3)], [(mine, mine, device(y=p)) for p in y_peers])

    def do_gc(e):
        full = of_part[e][6]
        arrive(("gy", e))
        mine = full.at[core]
        send(("gc", e), mine, [(mine, mine, device(core=other))])

    def do_up(e):
        h, start, width = PARTS[e]
        full = of_part[e][6]
        if ("fx",) in flying:
            arrive(("fx",))
        value = jnp.dot(
            rows_up[h, core].reshape(256, QUARTER), full[core].reshape(QUARTER, width),
            preferred_element_type=F32,
        )
        arrive(("gc", e))
        value = value + jnp.dot(
            rows_up[h, other].reshape(256, QUARTER), full[other].reshape(QUARTER, width),
            preferred_element_type=F32,
        )
        if h == 0:
            u_sum[:, pl.ds(start, width)] = value
        else:
            value = value + u_sum[:, pl.ds(start, width)]
            u_new[:, pl.ds(start, width)] = value.astype(BF)
            cols = pl.ds(start, width)
            cp = pltpu.make_async_copy(u_new.at[:, cols], u_out.at[:, cols], loc_sem.at[len(outs)])
            cp.start()
            outs.append(cp)

    steps = {
        "hop": do_hop, "zl": do_zl, "cnt": do_cnt, "mm": do_mm, "sx": do_sx,
        "sz": do_sz, "gx": do_gx, "turn": do_turn, "fz": do_fz, "fx": do_fx, "mm2": do_mm2,
        "sy": do_sy, "adam": do_adam, "gy": do_gy, "gc": do_gc, "up": do_up,
    }
    for name, *which in ORDER:
        steps[name](*which)

    @pl.when(moves)
    def _():
        for h in range(2):
            for c in range(2):
                hop_wait(h, c, send_sem)

    @pl.when(jnp.logical_not(moves))
    def _():
        for h in range(2):
            hop_wait(h, other, send_sem)

    for whole, i in groups:
        pltpu.make_async_copy(whole, whole, send_sem.at[i]).wait()
    for cp in outs:
        cp.wait()


def hand_on(m_in, v_in, u_in, m_out, v_out, u_out, m_held, v_held, u_held, sem):
    ways = ((m_in, m_held, m_out), (v_in, v_held, v_out), (u_in, u_held, u_out))
    reads = [pltpu.make_async_copy(a, b, sem.at[i]) for i, (a, b, _) in enumerate(ways)]
    writes = [pltpu.make_async_copy(b, c, sem.at[3 + i]) for i, (_, b, c) in enumerate(ways)]
    for cp in reads:
        cp.start()
    for read, write in zip(reads, writes):
        read.wait()
        write.start()
    for cp in writes:
        cp.wait()


def local(layer_input, out_grad, projector, first_moment, second_moment, doc_ids):
    scratch = [
        pltpu.VMEM((2, TOK, FEAT), BF),
        pltpu.VMEM((2, TOK, FF), BF),
        pltpu.VMEM((MOM, FF), F32),
        pltpu.VMEM((MOM, FF), F32),
        pltpu.VMEM((ROWS, RANK), BF),
        pltpu.VMEM((2, 2, 4, 4, ROWS, QUARTER), BF),
        pltpu.VMEM((2, 2, 4, 4, ROWS, QUARTER), BF),
        pltpu.VMEM((4, 4, 4, SUB, QUARTER), F32),
        pltpu.VMEM((4, 4, 4, SUB, QUARTER), BF),
        pltpu.VMEM((4, 3, 4, SUB, QUARTER), BF),
        pltpu.VMEM((4, 4, SUB, QUARTER), F32),
        pltpu.VMEM((4, 4, SUB, QUARTER), BF),
        pltpu.VMEM((4, 3, SUB, QUARTER), BF),
        pltpu.VMEM((4, 4, 4, SUB, QUARTER), BF),
        pltpu.VMEM((2, QUARTER, 2 * TOK), BF),
        pltpu.VMEM((3, 8, 128), F32),
        pltpu.VMEM((7, 8, 128), F32),
        pltpu.VMEM((2, 1, TOK), jnp.int32),
        pltpu.VMEM((256, FF), F32),
        pltpu.SemaphoreType.DMA((5,)),
        pltpu.SemaphoreType.DMA((N_SEM,)),
        pltpu.SemaphoreType.DMA((N_SEM,)),
    ]
    for _, _, w in PARTS:
        scratch += [
            pltpu.VMEM((4, 4, 16, w), F32),
            pltpu.VMEM((3, 4, 16, w), BF),
            pltpu.VMEM((3, 4, 16, w), BF),
            pltpu.VMEM((4, 16, w), F32),
            pltpu.VMEM((4, 16, w), BF),
            pltpu.VMEM((3, 16, w), BF),
            pltpu.VMEM((2, 4, 4, 16, w), BF),
        ]
    scratch += [
        pltpu.VMEM((MOM, FF), F32),
        pltpu.VMEM((MOM, FF), F32),
        pltpu.VMEM((256, FF), BF),
        pltpu.VMEM((2, 4, SUB, 128), F32),
    ]
    any_space = pl.BlockSpec(memory_space=pl.ANY)
    results = (
        jax.ShapeDtypeStruct((MOM, FF), F32),
        jax.ShapeDtypeStruct((MOM, FF), F32),
        jax.ShapeDtypeStruct((256, FF), BF),
    )
    made = pl.pallas_call(
        kernel,
        out_shape=results,
        in_specs=[any_space] * 5 + [pl.BlockSpec(memory_space=pltpu.VMEM)],
        out_specs=(any_space,) * 3,
        scratch_shapes=scratch,
        compiler_params=pltpu.CompilerParams(
            collective_id=0, has_side_effects=True, vmem_limit_bytes=56 * 2**20
        ),
        cost_estimate=pl.CostEstimate(flops=2 * 10**9, bytes_accessed=4 * 10**6, transcendentals=0),
        name="galore",
    )(layer_input, out_grad, projector, first_moment, second_moment, doc_ids.reshape(1, TOK))
    return pl.pallas_call(
        hand_on,
        out_shape=results,
        in_specs=[any_space] * 3,
        out_specs=(any_space,) * 3,
        scratch_shapes=[
            pltpu.VMEM((MOM, FF), F32),
            pltpu.VMEM((MOM, FF), F32),
            pltpu.VMEM((256, FF), BF),
            pltpu.SemaphoreType.DMA((6,)),
        ],
        compiler_params=pltpu.CompilerParams(vmem_limit_bytes=56 * 2**20),
        name="hand_on",
    )(*made)


def solution(mesh):
    placed = (
        P("dp", "shard"),
        P("dp", "shard"),
        P(("dp", "shard"), None),
        P("dp", "shard"),
        P("dp", "shard"),
        P("dp"),
    )
    return jax.shard_map(
        local,
        mesh=mesh,
        in_specs=placed,
        out_specs=(P("dp", "shard"), P("dp", "shard"), P("dp", "shard")),
        check_vma=False,
    )
```
